256 devices in a mesh: ctx: 16 (over x, z_lo), tp: 4 (over z_hi, core), dp: 4 (over y).
Axes of the slice: x: 4, y: 4, z: 8 (z_hi: 2, z_lo: 4; z = z_hi * 4 + z_lo), core: 2. Of those that a mesh axis runs over, the one named last changes fastest.
Arguments:
- trailing_questions: bfloat16 [8192, 8192], P(('dp', 'ctx'), 'tp'), parts along dimension 0, may hold values from -6 to 6
- output_gradient: bfloat16 [8192, 8192], P(('dp', 'ctx'), 'tp'), parts along dimension 0, may hold values from -6 to 6
- tail_row_key: bfloat16 [8192, 1024], P(('dp', 'ctx'), 'tp'), parts along dimension 0, may hold values from -6 to 6
- tail_row_value: bfloat16 [8192, 1024], P(('dp', 'ctx'), 'tp'), parts along dimension 0, may hold values from -6 to 6
- passage_key_cache: bfloat16 [16384, 1024], P(('dp', 'ctx'), 'tp'), parts along dimension 0, may hold values from -6 to 6
- passage_value_cache: bfloat16 [16384, 1024], P(('dp', 'ctx'), 'tp'), parts along dimension 0, may hold values from -6 to 6
- row_list: int32 [8192], P(('dp', 'ctx')), parts along dimension 0, may hold values from 0 to 1, as said below
- read_owner: int32 [64, 24], P(('dp', 'ctx')), parts along dimension 0, may hold values from 0 to 15, as said below
- read_tile: int32 [64, 24], P(('dp', 'ctx')), parts along dimension 0, may hold values from 0 to 1
- read_list: int32 [64, 24], P(('dp', 'ctx')), parts along dimension 0, may hold values from 0 to 1
- read_count: int32 [64], P(('dp', 'ctx')), parts along dimension 0, may hold values from 12 to 24, as said below
Outputs:
- grad_query: bfloat16 [8192, 8192], P(('dp', 'ctx'), 'tp'), parts along dimension 0
- grad_tail_key: bfloat16 [8192, 1024], P(('dp', 'ctx'), 'tp'), parts along dimension 0
- grad_tail_value: bfloat16 [8192, 1024], P(('dp', 'ctx'), 'tp'), parts along dimension 0
- grad_key_cache: float32 [16384, 1024], P(('dp', 'ctx'), 'tp'), parts along dimension 0
- grad_value_cache: float32 [16384, 1024], P(('dp', 'ctx'), 'tp'), parts along dimension 0
The draws below stay inside these ranges and needn't reach their ends.
There are 4 independent parts, one for each index of `dp`. The reference program is written for one: setup_inputs(seed, part) draws one part's arguments, and reference() takes and returns one part's arrays. A program takes and returns all parts, laid end to end along the dimension named above; each array names one. Nothing has to cross between parts.
Inputs may be any that keep to these rules, and one draw needn't show every extreme that they name: `row_list`: on each reader's 128 rows the list number is 0 on a first run and 1 on the rest; both runs are nonempty. `read_owner`: a reader names one owner at most 2 times, and every reader names some owner exactly 2 times. `read_count`: some reader has all 24 reads live.
All inputs are finite; a program needn't handle non-finite values.
Results may differ from the reference program's by a relative error of at most 0.012.
Values may be sent and summed in bfloat16 or wider, within the bound.
A program may use at most 64 MiB of HBM per device.

```python
import math
import jax
import jax.numpy as jnp
from jax import lax

QUERY_HEADS = 64
MEMORY_CHANNELS = 8
ATTN_WIDTH = 128
SUFFIX_LINES = 128
SEGMENT_FETCHES = 24
OWNED_TILES = 2
SEGMENT_LENGTH = 128
LISTS = 2
TAIL_ROWS = 2048
CACHED_TOKENS = 4096
N_CTX = 16


def draw_trailing_questions(key, part):
    query_group_size = QUERY_HEADS // MEMORY_CHANNELS
    complete_shape = (TAIL_ROWS, MEMORY_CHANNELS, query_group_size, ATTN_WIDTH)
    offset_start = jnp.clip(jax.random.normal(jax.random.fold_in(key, 1), complete_shape, jnp.float32), -6.0, 6.0)
    return offset_start.reshape(TAIL_ROWS, QUERY_HEADS * ATTN_WIDTH).astype(jnp.bfloat16)


def draw_tail_row_key(key, part):
    complete_shape = (TAIL_ROWS, MEMORY_CHANNELS, ATTN_WIDTH)
    offset_start = jnp.clip(jax.random.normal(jax.random.fold_in(key, 2), complete_shape, jnp.float32), -6.0, 6.0)
    return offset_start.reshape(TAIL_ROWS, MEMORY_CHANNELS * ATTN_WIDTH).astype(jnp.bfloat16)


def draw_row_list(key, part):
    cut_rows = jax.random.randint(jax.random.fold_in(key, 3), (N_CTX, 1), 1, SUFFIX_LINES)
    local_rows = jnp.arange(SUFFIX_LINES)[None, :]
    return (local_rows >= cut_rows).astype(jnp.int32).reshape(TAIL_ROWS)


def one_order(subkey):
    owner_order = jax.random.permutation(jax.random.fold_in(subkey, 1), N_CTX)
    column_order = jax.random.permutation(jax.random.fold_in(subkey, 2), SEGMENT_FETCHES)
    return owner_order[column_order % N_CTX]


def draw_read_owner(key, part):
    subkeys = jax.random.split(jax.random.fold_in(key, 4), N_CTX)
    return jax.vmap(one_order)(subkeys).astype(jnp.int32)


def draw_read_count(key, part):
    counts = jax.random.randint(jax.random.fold_in(key, 5), (N_CTX,), SEGMENT_FETCHES // 2, SEGMENT_FETCHES + 1)
    return jnp.where(jnp.arange(N_CTX) == 0, SEGMENT_FETCHES, counts).astype(jnp.int32)


def place_ends(array, key, smallest, largest):
    extent = array.shape
    spot = [jax.random.randint(jax.random.fold_in(key, axis), (), 0, extent[axis]) for axis in range(len(extent))]
    array = array.at[tuple(spot)].set(smallest)
    longest = extent.index(max(extent))
    spot[longest] = (spot[longest] + 1) % extent[longest]
    return array.at[tuple(spot)].set(largest)


def block_levels(stream_key, extent, shards, smallest, largest):
    level = 1.0
    for axis_at, shards_of in shards:
        steps = jax.random.uniform(jax.random.fold_in(jax.random.fold_in(stream_key, 6), axis_at), (shards_of,), jnp.float32, smallest / len(shards), largest / len(shards))
        level = level * jnp.repeat(jnp.exp(steps), extent[axis_at] // shards_of).reshape((-1,) + (1,) * (len(extent) - 1 - axis_at))
    return level


def bell_draw(key, shape, spread, reach, shards=(), dtype=jnp.bfloat16):
    array = jax.random.normal(key, shape, jnp.float32) * spread
    if len(shards) > 0:
        array = block_levels(key, shape, shards, -0.22, 0.18) * array
    return jnp.clip(array, min=-reach, max=reach).astype(dtype)


def setup_inputs(seed: int = 0, part: int = 0) -> dict:
    arg_keys = jax.random.split(jax.random.key(seed), 12)
    part_splits = jax.random.split(jax.random.fold_in(arg_keys[11], part), 12)
    trailing_questions = draw_trailing_questions(jax.random.fold_in(jax.random.fold_in(arg_keys[11], part), 71), part)
    output_gradient = bell_draw(part_splits[1], (TAIL_ROWS, QUERY_HEADS * ATTN_WIDTH), 1.0, 6.0, ((0, 16), (1, 4)))
    tail_row_key = draw_tail_row_key(jax.random.fold_in(jax.random.fold_in(arg_keys[11], part), 71), part)
    tail_row_value = bell_draw(part_splits[3], (TAIL_ROWS, MEMORY_CHANNELS * ATTN_WIDTH), 1.0, 6.0, ((0, 16), (1, 4)))
    passage_key_cache = bell_draw(part_splits[4], (CACHED_TOKENS, MEMORY_CHANNELS * ATTN_WIDTH), 1.0, 6.0, ((0, 16), (1, 4)))
    passage_value_cache = bell_draw(part_splits[5], (CACHED_TOKENS, MEMORY_CHANNELS * ATTN_WIDTH), 1.0, 6.0, ((0, 16), (1, 4)))
    row_list = draw_row_list(jax.random.fold_in(jax.random.fold_in(arg_keys[11], part), 71), part)
    read_owner = draw_read_owner(jax.random.fold_in(jax.random.fold_in(arg_keys[11], part), 71), part)
    read_tile = place_ends(jax.random.randint(part_splits[8], (N_CTX, SEGMENT_FETCHES), 0, OWNED_TILES), jax.random.fold_in(part_splits[8], 1), 0, OWNED_TILES - 1).astype(jnp.int32)
    read_list = place_ends(jax.random.randint(part_splits[9], (N_CTX, SEGMENT_FETCHES), 0, LISTS), jax.random.fold_in(part_splits[9], 1), 0, LISTS - 1).astype(jnp.int32)
    read_count = draw_read_count(jax.random.fold_in(jax.random.fold_in(arg_keys[11], part), 71), part)
    return {"trailing_questions": trailing_questions, "output_gradient": output_gradient, "tail_row_key": tail_row_key, "tail_row_value": tail_row_value, "passage_key_cache": passage_key_cache, "passage_value_cache": passage_value_cache, "row_list": row_list, "read_owner": read_owner, "read_tile": read_tile, "read_list": read_list, "read_count": read_count}


NEG_FILL = -1e+30

def reference(trailing_questions, output_gradient, tail_row_key, tail_row_value, passage_key_cache, passage_value_cache, row_list, read_owner, read_tile, read_list, read_count):
    query_group_size = QUERY_HEADS // MEMORY_CHANNELS
    sharpness_scale = 1.0 / math.sqrt(ATTN_WIDTH)
    stored_keys = passage_key_cache.reshape(N_CTX * OWNED_TILES, SEGMENT_LENGTH, MEMORY_CHANNELS, ATTN_WIDTH)
    stored_values = passage_value_cache.reshape(N_CTX * OWNED_TILES, SEGMENT_LENGTH, MEMORY_CHANNELS, ATTN_WIDTH)

    def one_reader(loop_accumulator, reader):
        running_keys, running_values = loop_accumulator
        begin_index = (reader * SUFFIX_LINES).astype(jnp.int32)
        asking_matrix = lax.dynamic_slice_in_dim(trailing_questions, begin_index, SUFFIX_LINES, 0).reshape(SUFFIX_LINES, MEMORY_CHANNELS, query_group_size, ATTN_WIDTH).astype(jnp.float32)
        result_cotangents = lax.dynamic_slice_in_dim(output_gradient, begin_index, SUFFIX_LINES, 0).reshape(SUFFIX_LINES, MEMORY_CHANNELS, query_group_size, ATTN_WIDTH).astype(jnp.float32)
        ending_keys = lax.dynamic_slice_in_dim(tail_row_key, begin_index, SUFFIX_LINES, 0).reshape(SUFFIX_LINES, MEMORY_CHANNELS, ATTN_WIDTH)
        ending_values = lax.dynamic_slice_in_dim(tail_row_value, begin_index, SUFFIX_LINES, 0).reshape(SUFFIX_LINES, MEMORY_CHANNELS, ATTN_WIDTH)
        own_list = lax.dynamic_slice_in_dim(row_list, begin_index, SUFFIX_LINES, 0)
        overall_tile = (read_owner[reader] * OWNED_TILES + read_tile[reader]).astype(jnp.int32)
        remote_keys = jnp.take(stored_keys, overall_tile, axis=0).reshape(SEGMENT_FETCHES * SEGMENT_LENGTH, MEMORY_CHANNELS, ATTN_WIDTH)
        remote_values = jnp.take(stored_values, overall_tile, axis=0).reshape(SEGMENT_FETCHES * SEGMENT_LENGTH, MEMORY_CHANNELS, ATTN_WIDTH)
        every_address_vector = jnp.concatenate([ending_keys, remote_keys], axis=0).astype(jnp.float32)
        all_values = jnp.concatenate([ending_values, remote_values], axis=0).astype(jnp.float32)
        positions = jnp.arange(SUFFIX_LINES)
        tail_allowed = (own_list[:, None] == own_list[None, :]) & (positions[None, :] <= positions[:, None])
        key_lists = jnp.repeat(read_list[reader], SEGMENT_LENGTH)
        key_live = jnp.repeat(jnp.arange(SEGMENT_FETCHES) < read_count[reader], SEGMENT_LENGTH)
        far_allowed = (own_list[:, None] == key_lists[None, :]) & key_live[None, :]
        permitted_mask = jnp.concatenate([tail_allowed, far_allowed], axis=1)
        similarity_matrix = jnp.einsum('sjvf,ijf->jvsi', asking_matrix, every_address_vector) * sharpness_scale
        similarity_matrix = jnp.where(permitted_mask[None, None], similarity_matrix, NEG_FILL)
        row_max = lax.optimization_barrier(jnp.max(similarity_matrix, axis=-1, keepdims=True))
        log_norm = row_max + jnp.log(lax.optimization_barrier(jnp.sum(jnp.exp(similarity_matrix - row_max), axis=-1, keepdims=True)))
        attn_prob = jnp.exp(similarity_matrix - log_norm)
        dprob = jnp.einsum('sjvf,ijf->jvsi', result_cotangents, all_values)
        delta = lax.optimization_barrier(jnp.sum(attn_prob * dprob, axis=-1, keepdims=True))
        dscore = attn_prob * (dprob - delta)
        softmax_weights_lowp = lax.optimization_barrier(attn_prob.astype(jnp.bfloat16)).astype(jnp.float32)
        score_adjoint_halfprec = lax.optimization_barrier(dscore.astype(jnp.bfloat16)).astype(jnp.float32)
        derivative_lines_matrix = (jnp.einsum('ctba,aci->bcti', score_adjoint_halfprec, every_address_vector) * sharpness_scale).astype(jnp.bfloat16)
        retrieval_shares = (jnp.einsum('frjc,jfrx->cfx', score_adjoint_halfprec, asking_matrix) * sharpness_scale).astype(jnp.bfloat16)
        content_contributions = jnp.einsum('frjc,jfrx->cfx', softmax_weights_lowp, result_cotangents).astype(jnp.bfloat16)
        final_lookup_cotangent = retrieval_shares[:SUFFIX_LINES].reshape(SUFFIX_LINES, MEMORY_CHANNELS * ATTN_WIDTH)
        final_content_cotangent = content_contributions[:SUFFIX_LINES].reshape(SUFFIX_LINES, MEMORY_CHANNELS * ATTN_WIDTH)
        distant_lookup_cotangent = retrieval_shares[SUFFIX_LINES:].reshape(SEGMENT_FETCHES, SEGMENT_LENGTH, MEMORY_CHANNELS, ATTN_WIDTH).astype(jnp.float32)
        distant_content_cotangent = content_contributions[SUFFIX_LINES:].reshape(SEGMENT_FETCHES, SEGMENT_LENGTH, MEMORY_CHANNELS, ATTN_WIDTH).astype(jnp.float32)
        read_index = jnp.arange(SEGMENT_FETCHES)
        same_tile = overall_tile[:, None] == overall_tile[None, :]
        earlier = read_index[None, :] < read_index[:, None]
        first_read = jnp.logical_not(jnp.any(same_tile & earlier, axis=1)).astype(jnp.float32)
        same_float = same_tile.astype(jnp.float32)
        summed_k = jnp.einsum('st,tkhd->skhd', same_float, distant_lookup_cotangent).astype(jnp.bfloat16).astype(jnp.float32)
        summed_v = jnp.einsum('st,tkhd->skhd', same_float, distant_content_cotangent).astype(jnp.bfloat16).astype(jnp.float32)
        summed_k = summed_k * first_read[:, None, None, None]
        summed_v = summed_v * first_read[:, None, None, None]
        running_keys = running_keys.at[overall_tile].add(summed_k)
        running_values = running_values.at[overall_tile].add(summed_v)
        return ((running_keys, running_values), (derivative_lines_matrix.reshape(SUFFIX_LINES, QUERY_HEADS * ATTN_WIDTH), final_lookup_cotangent, final_content_cotangent))
    initial_zeros = jnp.zeros((N_CTX * OWNED_TILES, SEGMENT_LENGTH, MEMORY_CHANNELS, ATTN_WIDTH), jnp.float32)
    (running_keys, running_values), (derivative_lines_matrix, final_lookup_cotangent, final_content_cotangent) = lax.scan(one_reader, (initial_zeros, initial_zeros), jnp.arange(N_CTX).astype(jnp.int32))
    return (derivative_lines_matrix.reshape(TAIL_ROWS, QUERY_HEADS * ATTN_WIDTH), final_lookup_cotangent.reshape(TAIL_ROWS, MEMORY_CHANNELS * ATTN_WIDTH), final_content_cotangent.reshape(TAIL_ROWS, MEMORY_CHANNELS * ATTN_WIDTH), running_keys.reshape(CACHED_TOKENS, MEMORY_CHANNELS * ATTN_WIDTH), running_values.reshape(CACHED_TOKENS, MEMORY_CHANNELS * ATTN_WIDTH))
```

```python
import functools
import math

import jax
import jax.numpy as jnp
from jax import lax
from jax.experimental import pallas as pl
from jax.experimental.pallas import tpu as pltpu
from jax.sharding import PartitionSpec as P

W = 128
NX = 4
NZ = 4
SCALE = 1.0 / math.sqrt(W)
LOG2E = 1.4426950408889634
SCORE_TO_LOG2 = SCALE * LOG2E
MASKED = -1e30
FLOOR = -1e29
NB = 256
f32 = jnp.float32
bf16 = jnp.bfloat16
MESH = pl.DeviceIdType.MESH
TT = (((0,), (0,)), ((), ()))


def kernel(
    q_ref, do_ref, tk_ref, tv_ref, kc_ref, vc_ref, rl_ref, ro_ref, rt_ref, rs_ref, rc_ref,
    gq_ref, gk_ref, gv_ref, gck_ref, gcv_ref,
    G, GR, R1, R2, RZ2, RZ, QR, DR, QT, DT, m_ref, l_ref, c_ref, bias_ref, dq_ref, pb, db,
    a_recv, a_send_x, a_send_zi, a_send_zo,
    r1_recv, r1_send, r2_recv, r2_send, rz2_recv, rz2_send, rz_recv, rz_send,
):
    me = lax.axis_index("ctx")
    x = me // NZ
    z = me % NZ
    xp = lax.rem(x + 1, NX)
    xm = lax.rem(x + NX - 1, NX)
    x2 = lax.rem(x + 2, NX)
    inner = (z == 1) | (z == 2)
    edge = (z == 0) | (z == 3)
    low = z < 2
    zi = jnp.where(low, z + 1, z - 1)
    zo = jnp.where(low, z - 1, z + 1)
    to_xp = xp * NZ + z
    to_xm = xm * NZ + z
    to_zi = x * NZ + zi
    to_zo = x * NZ + zo
    zk = [z, jnp.where(lax.rem(z, 2) == 0, z + 1, z - 1), jnp.where(low, 2, 1), jnp.where(low, 3, 0)]

    def when(cond, fn):
        if cond is None:
            fn()
        else:
            pl.when(cond)(fn)

    def send(src, dst, ssem, rsem, dev):
        pltpu.make_async_remote_copy(
            src_ref=src, dst_ref=dst, send_sem=ssem, recv_sem=rsem, device_id={"ctx": dev}, device_id_type=MESH
        ).start()

    def wait_recv(dst, rsem):
        pltpu.make_async_remote_copy(
            src_ref=dst, dst_ref=dst, send_sem=rsem, recv_sem=rsem, device_id={"ctx": to_xp}, device_id_type=MESH
        ).wait_recv()

    def wait_send(src, ssem):
        pltpu.make_async_remote_copy(
            src_ref=src, dst_ref=src, send_sem=ssem, recv_sem=ssem, device_id={"ctx": to_xp}, device_id_type=MESH
        ).wait_send()

    barrier = pltpu.get_barrier_semaphore()

    def greet(dev):
        pl.semaphore_signal(barrier, inc=1, device_id={"ctx": dev}, device_id_type=MESH)

    greet(to_xp)
    greet(to_xm)
    greet(to_zi)
    when(inner, lambda: greet(to_zo))

    for a in range(2):
        G[me, a, 0] = kc_ref[a * W : (a + 1) * W, :]
        G[me, a, 1] = vc_ref[a * W : (a + 1) * W, :]

    when(inner, lambda: pl.semaphore_wait(barrier, 4))
    when(edge, lambda: pl.semaphore_wait(barrier, 3))

    def a_x(owner, k, a, dirs=(0, 1), slot=None):
        for d in dirs:
            send(
                G.at[owner, a], G.at[owner, a], a_send_x.at[d, k, a if slot is None else slot], a_recv.at[owner, a],
                (to_xp, to_xm)[d],
            )

    def a_zi(owner, k, a):
        send(G.at[owner, a], G.at[owner, a], a_send_zi.at[k, a], a_recv.at[owner, a], to_zi)

    def a_zo(owner, k, a):
        send(G.at[owner, a], G.at[owner, a], a_send_zo.at[k, a], a_recv.at[owner, a], to_zo)

    for a in range(2):
        a_zi(me, 0, a)
        when(inner, functools.partial(a_zo, me, 0, a))
        a_x(me, 0, a)

    for h in range(2):
        for j in range(8):
            cols = slice((h * 8 + j) * W, (h * 8 + j + 1) * W)
            rows = slice(j * W, (j + 1) * W)
            qb = q_ref[:, cols]
            ob = do_ref[:, cols]
            QR[h, rows, :] = qb
            DR[h, rows, :] = ob
            QT[h, :, rows] = qb.T
            DT[h, :, rows] = ob.T
    reads = ro_ref.shape[1]
    tid = ro_ref[...] * 2 + rt_ref[...]
    live = lax.broadcasted_iota(jnp.int32, (1, reads), 1) < rc_ref[...]
    tid = jnp.where(live, tid, -1)
    named = lax.broadcasted_iota(jnp.int32, (2 * NX * NZ, reads), 0) == tid
    count0 = jnp.sum(jnp.where(named & (rs_ref[...] == 0), 1.0, 0.0), axis=1, keepdims=True)
    count1 = jnp.sum(jnp.where(named & (rs_ref[...] == 1), 1.0, 0.0), axis=1, keepdims=True)
    rl = rl_ref[...]
    times = jnp.where(rl == 0, count0, count1)
    bias_ref[...] = jnp.where(times > 0.5, jnp.log2(jnp.maximum(times, 1.0)), MASKED)
    cut = jnp.sum(jnp.where(rl == 0, 1.0, 0.0), axis=1, keepdims=True)
    key_at = lax.broadcasted_iota(jnp.int32, (W, W), 0)
    row_at = lax.broadcasted_iota(jnp.int32, (W, W), 1)
    tail_ok = (key_at <= row_at) & jnp.logical_not((key_at.astype(f32) < cut) & (row_at.astype(f32) >= cut))
    tail_ok = jnp.concatenate([tail_ok.astype(f32)] * (NB // W), axis=1) > 0.5

    for h in range(2):
        hs = slice(h * W, (h + 1) * W)
        for j in range(8 * W // NB):
            sl = slice(j * NB, (j + 1) * NB)
            s = jnp.dot(tk_ref[:, hs], QT[h, :, sl], preferred_element_type=f32)
            dp = jnp.dot(tv_ref[:, hs], DT[h, :, sl], preferred_element_type=f32)
            t = jnp.where(tail_ok, s * SCORE_TO_LOG2, MASKED).reshape(16, 8, NB)
            top = jnp.maximum(jnp.max(t, axis=0), FLOOR)
            e = jnp.exp2(t - top[None])
            m_ref[h, :, sl] = top
            l_ref[h, :, sl] = jnp.sum(e, axis=0)
            c_ref[h, :, sl] = jnp.sum(e * dp.reshape(16, 8, NB), axis=0)

    def tile_bias(owner, a):
        b = jnp.broadcast_to(bias_ref[pl.ds(owner * 2 + a, 1), :], (8, W))
        return jnp.concatenate([b] * (NB // W), axis=1)

    def stats_chunk(owner):
        for a in range(2):
            b = tile_bias(owner, a)
            for h in range(2):
                hs = slice(h * W, (h + 1) * W)
                for j in range(8 * W // NB):
                    sl = slice(j * NB, (j + 1) * NB)
                    s = jnp.dot(G[owner, a, 0, :, hs], QT[h, :, sl], preferred_element_type=f32)
                    dp = jnp.dot(G[owner, a, 1, :, hs], DT[h, :, sl], preferred_element_type=f32)
                    t = (s * SCORE_TO_LOG2).reshape(16, 8, NB)
                    old = m_ref[h, :, sl]
                    new = jnp.maximum(old, jnp.max(t, axis=0) + b)
                    fade = jnp.exp2(old - new)
                    e = jnp.exp2(t - (new - b)[None])
                    m_ref[h, :, sl] = new
                    l_ref[h, :, sl] = l_ref[h, :, sl] * fade + jnp.sum(e, axis=0)
                    c_ref[h, :, sl] = c_ref[h, :, sl] * fade + jnp.sum(e * dp.reshape(16, 8, NB), axis=0)

    def got_a(k):
        owner = x * NZ + zk[k]
        for a in range(2):
            wait_recv(G.at[owner, a], a_recv.at[owner, a])
            when(inner, functools.partial(a_zi if k == 1 else a_zo, owner, k, a))
            a_x(owner, k, a)

    def got_b(k):
        right = xp * NZ + zk[k]
        left = xm * NZ + zk[k]
        wait_recv(G.at[left, 0], a_recv.at[left, 0])
        if k < 2:
            a_x(left, k, 0, (0,), 2)
        wait_recv(G.at[right, 0], a_recv.at[right, 0])
        wait_recv(G.at[right, 1], a_recv.at[right, 1])
        if k < 2:
            a_x(right, k, 1, (1,), 2)
        wait_recv(G.at[left, 1], a_recv.at[left, 1])

    def got_c(k):
        owner = x2 * NZ + zk[k]
        for a in range(2):
            wait_recv(G.at[owner, a], a_recv.at[owner, a])
            if k < 2:
                when(inner, functools.partial(a_zi, owner, k + 2, a))
            else:
                when(inner, functools.partial(a_zo, owner, k + 2, a))

    gather_plan = [
        (x * NZ + zk[0], None),
        (x * NZ + zk[1], lambda: got_a(1)),
        (xp * NZ + zk[0], lambda: got_b(0)),
        (xm * NZ + zk[0], None),
        (x * NZ + zk[2], lambda: got_a(2)),
        (xp * NZ + zk[1], lambda: got_b(1)),
        (xm * NZ + zk[1], None),
        (x2 * NZ + zk[0], lambda: got_c(0)),
        (x * NZ + zk[3], lambda: got_a(3)),
        (x2 * NZ + zk[1], lambda: got_c(1)),
        (xp * NZ + zk[2], lambda: got_b(2)),
        (xm * NZ + zk[2], None),
        (xp * NZ + zk[3], lambda: got_b(3)),
        (xm * NZ + zk[3], None),
        (x2 * NZ + zk[2], lambda: got_c(2)),
        (x2 * NZ + zk[3], lambda: got_c(3)),
    ]

    def gather_step(n, carry):
        owner = jnp.int32(0)
        for at, (own, act) in enumerate(gather_plan):
            owner = jnp.where(n == at, own, owner)
            if act is not None:
                pl.when(n == at)(act)
        stats_chunk(owner)
        return carry

    lax.fori_loop(0, len(gather_plan), gather_step, 0)

    for h in range(2):
        m = m_ref[h]
        top = jnp.max(m, axis=0, keepdims=True)
        part = jnp.exp2(m - top)
        total = jnp.sum(l_ref[h] * part, axis=0, keepdims=True)
        cross = jnp.sum(c_ref[h] * part, axis=0, keepdims=True)
        m_ref[h] = jnp.broadcast_to(top + jnp.log2(total), (8, 8 * W))
        c_ref[h] = jnp.broadcast_to(cross / total, (8, 8 * W))
        dq_ref[h] = jnp.zeros((W, 8 * W), f32)

    def grads_chunk(owner):
        for h in range(2):
            hs = slice(h * W, (h + 1) * W)
            for a in range(2):
                b = tile_bias(owner, a)
                rows = slice(a * W, (a + 1) * W)
                for j in range(8 * W // NB):
                    sl = slice(j * NB, (j + 1) * NB)
                    s = jnp.dot(G[owner, a, 0, :, hs], QT[h, :, sl], preferred_element_type=f32)
                    dp = jnp.dot(G[owner, a, 1, :, hs], DT[h, :, sl], preferred_element_type=f32)
                    p = jnp.exp2((s * SCORE_TO_LOG2).reshape(16, 8, NB) - (m_ref[h, :, sl] - b)[None])
                    d = p * (dp.reshape(16, 8, NB) - c_ref[h, :, sl][None])
                    pb[h, rows, sl] = p.reshape(W, NB).astype(bf16)
                    db[h, rows, sl] = d.reshape(W, NB).astype(bf16)
            dv = jnp.dot(pb[h], DR[h], preferred_element_type=f32)
            dk = jnp.dot(db[h], QR[h], preferred_element_type=f32) * SCALE
            for a in range(2):
                rows = slice(a * W, (a + 1) * W)
                GR[owner, a, 0, :, hs] = dk[rows].astype(bf16)
                GR[owner, a, 1, :, hs] = dv[rows].astype(bf16)
            keys = jnp.concatenate([G[owner, 0, 0, :, hs], G[owner, 1, 0, :, hs]], axis=0)
            dq_ref[h] += lax.dot_general(keys, db[h], TT, preferred_element_type=f32)

    def merge(ref, parts):
        def rows_of(i, carry):
            r = pl.ds(pl.multiple_of(i * 32, 32), 32)
            total = ref[:, r, :].astype(f32)
            for part in parts:
                total = total + part[:, r, :].astype(f32)
            ref[:, r, :] = total.astype(bf16)
            return carry

        lax.fori_loop(0, W // 32, rows_of, 0)

    def r1(d, k, a):
        owner = (xm if d == 0 else xp) * NZ + zk[k]
        send(GR.at[owner, a], R1.at[d, k, a], r1_send.at[d, k, a], r1_recv.at[d, k, a], (to_xm, to_xp)[d])

    def r1_both(d, k):
        r1(d, k, 0)
        r1(d, k, 1)

    def r2(k):
        owner = x2 * NZ + zk[k]
        for a in range(2):
            send(GR.at[owner, a], R2.at[k, a], r2_send.at[k, a], r2_recv.at[k, a], (to_xm, to_xp)[a])

    def r2_merged(k):
        def fn():
            owner = x2 * NZ + zk[k]
            for a in range(2):
                wait_recv(RZ2.at[k, a], rz2_recv.at[k, a])
                merge(GR.at[owner, a], [RZ2.at[k, a]])
            r2(k)

        return fn

    def rz2_edge(k):
        def fn():
            owner = x2 * NZ + zk[k]
            for a in range(2):
                send(GR.at[owner, a], RZ2.at[k, a], rz2_send.at[k - 2, a], rz2_recv.at[k, a], to_zi)

        return fn

    def rz2_inner(k):
        def fn():
            owner = x2 * NZ + zk[k]
            for a in range(2):
                wait_recv(RZ2.at[k, a], rz2_recv.at[k, a])
                merge(GR.at[owner, a], [RZ2.at[k, a]])
                send(GR.at[owner, a], RZ2.at[k - 2, a], rz2_send.at[k - 2, a], rz2_recv.at[k - 2, a], to_zi)

        return fn

    def r1_merged(k):
        for d in range(2):
            a = d
            owner = (xm if d == 0 else xp) * NZ + zk[k]
            wait_recv(R2.at[k, a], r2_recv.at[k, a])
            merge(GR.at[owner, a], [R2.at[k, a]])
            r1(d, k, a)

    def got_r1(k, a):
        for d in range(2):
            wait_recv(R1.at[d, k, a], r1_recv.at[d, k, a])

    def rz_edge(k):
        def fn():
            owner = x * NZ + zk[k]
            slot = 4 if k == 1 else k
            for a in range(2):
                got_r1(k, a)
                merge(GR.at[owner, a], [R1.at[0, k, a], R1.at[1, k, a]])
                send(GR.at[owner, a], RZ.at[slot, a], rz_send.at[k - 1, a], rz_recv.at[slot, a], to_zi)

        return fn

    def rz_inner(k):
        def fn():
            owner = x * NZ + zk[k]
            slot = 0 if k == 1 else k - 2
            for a in range(2):
                got_r1(k, a)
                wait_recv(RZ.at[k, a], rz_recv.at[k, a])
                merge(GR.at[owner, a], [R1.at[0, k, a], R1.at[1, k, a], RZ.at[k, a]])
                send(GR.at[owner, a], RZ.at[slot, a], rz_send.at[k - 1, a], rz_recv.at[slot, a], to_zo if k == 1 else to_zi)

        return fn

    plan = {n: [] for n in range(16)}
    plan[0] += [(edge, rz2_edge(3))]
    plan[1] += [(None, lambda: r1_both(0, 3))]
    plan[2] += [(None, lambda: r1_both(1, 3))]
    plan[4] += [(edge, rz2_edge(2))]
    plan[5] += [(None, lambda: r1_both(0, 2)), (inner, rz2_inner(3))]
    plan[6] += [(None, lambda: r1_both(1, 2))]
    plan[7] += [(edge, rz_edge(3))]
    plan[8] += [(edge, lambda: r2(1)), (inner, rz2_inner(2))]
    plan[9] += [(None, lambda: r1(0, 1, 1))]
    plan[10] += [(None, lambda: r1(1, 1, 0)), (inner, r2_merged(1))]
    plan[11] += [(edge, rz_edge(2)), (inner, rz_inner(3))]
    plan[12] += [(edge, lambda: r2(0)), (None, lambda: r1_merged(1))]
    plan[13] += [(None, lambda: r1(0, 0, 1)), (inner, r2_merged(0))]
    plan[14] += [(None, lambda: r1(1, 0, 0)), (inner, rz_inner(2))]
    plan[15] += [(None, lambda: r1_merged(0))]

    def scatter_step(n, carry):
        kind = lax.rem(n, 4)
        at = n // 4
        zs = jnp.where(at == 0, zk[3], jnp.where(at == 1, zk[2], jnp.where(at == 2, zk[1], zk[0])))
        xs = jnp.where(kind == 0, x2, jnp.where(kind == 1, xm, jnp.where(kind == 2, xp, x)))
        grads_chunk(xs * NZ + zs)
        for step, acts in plan.items():
            if acts:

                def run(acts=acts):
                    for cond, act in acts:
                        when(cond, act)

                pl.when(n == step)(run)
        return carry

    lax.fori_loop(0, 16, scatter_step, 0)

    for h in range(2):
        hs = slice(h * W, (h + 1) * W)
        for j in range(8 * W // NB):
            sl = slice(j * NB, (j + 1) * NB)
            s = jnp.dot(tk_ref[:, hs], QT[h, :, sl], preferred_element_type=f32)
            dp = jnp.dot(tv_ref[:, hs], DT[h, :, sl], preferred_element_type=f32)
            t = jnp.where(tail_ok, s * SCORE_TO_LOG2, MASKED).reshape(16, 8, NB)
            p = jnp.exp2(t - m_ref[h, :, sl][None])
            d = p * (dp.reshape(16, 8, NB) - c_ref[h, :, sl][None])
            pb[h, :W, sl] = p.reshape(W, NB).astype(bf16)
            db[h, :W, sl] = d.reshape(W, NB).astype(bf16)
        gv_ref[:, hs] = jnp.dot(pb[h, :W, :], DR[h], preferred_element_type=f32).astype(bf16)
        gk_ref[:, hs] = (jnp.dot(db[h, :W, :], QR[h], preferred_element_type=f32) * SCALE).astype(bf16)
        dq_ref[h] += lax.dot_general(tk_ref[:, hs], db[h, :W, :], TT, preferred_element_type=f32)

    when(edge, rz_edge(1))
    when(inner, rz_inner(1))

    for h in range(2):
        for j in range(8):
            gq_ref[:, (h * 8 + j) * W : (h * 8 + j + 1) * W] = (
                (dq_ref[h, :, j * W : (j + 1) * W] * SCALE).T.astype(bf16)
            )

    for a in range(2):
        rows = slice(a * W, (a + 1) * W)
        got_r1(0, a)
        wait_recv(RZ.at[0, a], rz_recv.at[0, a])
        for i, out in enumerate((gck_ref, gcv_ref)):
            out[rows, :] = (
                GR[me, a, i].astype(f32)
                + R1[0, 0, a, i].astype(f32)
                + R1[1, 0, a, i].astype(f32)
                + RZ[0, a, i].astype(f32)
            )

        def add_outer(a=a, rows=rows):
            wait_recv(RZ.at[4, a], rz_recv.at[4, a])
            for i, out in enumerate((gck_ref, gcv_ref)):
                out[rows, :] += RZ[4, a, i].astype(f32)

        when(inner, add_outer)

    tile = G.at[0, 0]
    for a in range(2):
        for k in range(4):
            wait_send(tile, a_send_x.at[0, k, a])
            wait_send(tile, a_send_x.at[1, k, a])
            wait_send(tile, r1_send.at[0, k, a])
            wait_send(tile, r1_send.at[1, k, a])
        for k in range(2):
            wait_send(tile, r2_send.at[k, a])
            wait_send(tile, rz2_send.at[k, a])
            wait_send(tile, a_send_x.at[a, k, 2])
        for k in range(3):
            wait_send(tile, rz_send.at[k, a])
        wait_send(tile, a_send_zi.at[0, a])

        def inner_sends(a=a):
            for k in (1, 2, 3):
                wait_send(tile, a_send_zi.at[k, a])
            for k in (0, 2, 3, 4, 5):
                wait_send(tile, a_send_zo.at[k, a])

        when(inner, inner_sends)


def body(q, do, tk, tv, kc, vc, row_list, read_owner, read_tile, read_list, read_count):
    rows, width = q.shape
    kv_width = tk.shape[1]
    groups = width // kv_width
    vmem = pl.BlockSpec(memory_space=pltpu.VMEM)
    tile = (2, W, kv_width)
    dma = pltpu.SemaphoreType.DMA
    scratch = [
        pltpu.VMEM((NX * NZ, 2) + tile, bf16),
        pltpu.VMEM((NX * NZ, 2) + tile, bf16),
        pltpu.VMEM((2, 4, 2) + tile, bf16),
        pltpu.VMEM((2, 2) + tile, bf16),
        pltpu.VMEM((4, 2) + tile, bf16),
        pltpu.VMEM((5, 2) + tile, bf16),
        pltpu.VMEM((2, groups * W, W), bf16),
        pltpu.VMEM((2, groups * W, W), bf16),
        pltpu.VMEM((2, W, groups * W), bf16),
        pltpu.VMEM((2, W, groups * W), bf16),
        pltpu.VMEM((2, 8, groups * W), f32),
        pltpu.VMEM((2, 8, groups * W), f32),
        pltpu.VMEM((2, 8, groups * W), f32),
        pltpu.VMEM((2 * NX * NZ, W), f32),
        pltpu.VMEM((2, W, groups * W), f32),
        pltpu.VMEM((2, 2 * W, groups * W), bf16),
        pltpu.VMEM((2, 2 * W, groups * W), bf16),
        dma((NX * NZ, 2)),
        dma((2, 4, 3)),
        dma((4, 2)),
        dma((6, 2)),
        dma((2, 4, 2)),
        dma((2, 4, 2)),
        dma((2, 2)),
        dma((2, 2)),
        dma((4, 2)),
        dma((2, 2)),
        dma((5, 2)),
        dma((3, 2)),
    ]
    pairs = 2 * groups * rows * (2 * NX * NZ + 1) * W * W * 2
    return pl.pallas_call(
        kernel,
        name="tail_attention_backward",
        out_shape=(
            jax.ShapeDtypeStruct((rows, width), bf16),
            jax.ShapeDtypeStruct((rows, kv_width), bf16),
            jax.ShapeDtypeStruct((rows, kv_width), bf16),
            jax.ShapeDtypeStruct(kc.shape, f32),
            jax.ShapeDtypeStruct(vc.shape, f32),
        ),
        in_specs=[vmem] * 11,
        out_specs=(vmem,) * 5,
        scratch_shapes=scratch,
        cost_estimate=pl.CostEstimate(flops=7 * pairs, bytes_accessed=4 << 20, transcendentals=pairs // W),
        compiler_params=pltpu.CompilerParams(
            collective_id=0, has_side_effects=True, vmem_limit_bytes=48 << 20
        ),
    )(
        q, do, tk, tv, kc, vc,
        row_list.reshape(1, rows), read_owner, read_tile, read_list, read_count.reshape(1, 1),
    )


def solution(mesh):
    split = P(("dp", "ctx"), "tp")
    per_ctx = P(("dp", "ctx"), None)
    flat = P(("dp", "ctx"))
    return jax.shard_map(
        body,
        mesh=mesh,
        in_specs=(split,) * 6 + (flat, per_ctx, per_ctx, per_ctx, flat),
        out_specs=(split,) * 5,
        check_vma=False,
    )
```

```python
import functools
import math

import jax
import jax.numpy as jnp
from jax import lax
from jax.experimental import pallas as pl
from jax.experimental.pallas import tpu as pltpu
from jax.sharding import PartitionSpec as P

W = 128
NX = 4
NZ = 4
SCALE = 1.0 / math.sqrt(W)
LOG2E = 1.4426950408889634
SCORE_TO_LOG2 = SCALE * LOG2E
MASKED = -1e30
FLOOR = -1e29
NB = 256
f32 = jnp.float32
bf16 = jnp.bfloat16
MESH = pl.DeviceIdType.MESH
TT = (((0,), (0,)), ((), ()))

GATHER = (
    (
        (("A000", "A001", "A002", "A010", "A011", "A012",), "A00"),
        ((), "A01"),
        (("A10w", "P00w", "M00w", "A100", "A101",), "A10"),
        ((), "P00"),
        ((), "M00"),
        (("A11w", "P01w", "M01w", "A110", "A111",), "A11"),
        ((), "P01"),
        ((), "M01"),
        (("A20w", "P10w", "M10w", "A200", "A201",), "A20"),
        ((), "P10"),
        ((), "M10"),
        (("A21w", "P11w", "M11w", "A210", "A211",), "A21"),
        ((), "P11"),
        ((), "M11"),
        (("A30w", "P20w", "M20w", "A300", "A301",), "A30"),
        ((), "P20"),
        ((), "M20"),
        (("A31w", "P21w", "M21w", "M000", "M100", "A310", "A311", "P011", "P111",), "A31"),
        ((), "P21"),
        ((), "M21"),
        (("C20w", "P30w", "M30w",), "C20"),
        ((), "P30"),
        ((), "M30"),
        (("C21w", "P31w", "M31w",), "C21"),
        ((), "P31"),
        ((), "M31"),
        (("C30w", "C00w", "C01w",), "C30"),
        ((), "C00"),
        ((), "C01"),
        (("C10w", "C31w", "C11w",), "C10"),
        ((), "C31"),
        ((), "C11"),
    ),
    (
        (("A002", "A000", "A001", "A003", "A012", "A010", "A011", "A013",), "A00"),
        ((), "A01"),
        (("A10w", "A20w", "P00w", "M00w", "A102", "M000", "A100", "A101", "A203",), "A10"),
        ((), "A20"),
        ((), "P00"),
        ((), "M00"),
        (("A11w", "A21w", "P01w", "M01w", "A201", "A112", "A110", "P011", "A111", "A213",), "A11"),
        ((), "A21"),
        ((), "P01"),
        ((), "M01"),
        (("A30w", "P10w", "C00w", "C002", "A303",), "A30"),
        ((), "P10"),
        ((), "C00"),
        (("M10w", "A31w", "C01w", "M100", "A200", "A300", "C012", "A210", "A310", "A313",), "M10"),
        ((), "A31"),
        ((), "C01"),
        (("C20w", "P11w", "M11w", "A301", "C203", "P111", "A211", "A311",), "C20"),
        ((), "P11"),
        ((), "M11"),
        (("P20w", "C10w", "C21w", "C102", "C213",), "P20"),
        ((), "C10"),
        ((), "C21"),
        (("M20w", "C11w", "C112",), "M20"),
        ((), "C11"),
        (("C30w", "C303",), "C30"),
        (("P21w", "M21w",), "P21"),
        ((), "M21"),
        (("C31w", "C313",), "C31"),
        (("P30w", "M30w",), "P30"),
        ((), "M30"),
        (("P31w", "M31w",), "P31"),
        ((), "M31"),
    ),
)
SCATTER = (
    (
        ("23", ()),
        ("m3", ()),
        ("21", ()),
        ("22", ()),
        ("p3", ()),
        ("p2", ()),
        ("m2", ()),
        ("p1", ("p11",)),
        ("01", ()),
        ("03", ("030",)),
        ("20", ()),
        ("m1", ("m10", "031",)),
        ("p0", ()),
        ("m0", ()),
        ("02", ("020",)),
        ("00", ()),
        ("T0", ("021",)),
        ("U0", ("m00", "011", "010", "p01", "000", "001",)),
    ),
    (
        ("m3", ()),
        ("p0", ()),
        ("p3", ()),
        ("m0", ()),
        ("23", ("230",)),
        ("21", ()),
        ("03", ()),
        ("01", ("231",)),
        ("p2", ("210",)),
        ("m1", ()),
        ("m2", ()),
        ("22", ("211", "220", "221",)),
        ("02", ("m10",)),
        ("p1", ()),
        ("20", ("030",)),
        ("00", ("200",)),
        ("T0", ("031",)),
        ("U0", ("p11", "201", "020", "021", "010", "011", "m00", "p01", "000", "001",)),
    ),
)


def kernel(
    q_hbm, do_hbm, tk_hbm, tv_hbm, kc_hbm, vc_hbm, rl_hbm, ro_hbm, rt_hbm, rs_hbm, rc_hbm,
    gq_hbm, gk_hbm, gv_hbm, gck_hbm, gcv_hbm,
    gq_ref, gk_ref, gv_ref, gck_ref, gcv_ref, tk_ref, tv_ref, rl_ref, ro_ref, rt_ref, rs_ref, rc_ref,
    G, GR, R1, R2, RZ2, RZ, QR, DR, QT, DT, m_ref, l_ref, c_ref, shift_ref, bias_ref, dq_ref, PS, DS, top_ref,
    in_sem, q_sem, out_sem, a_recv, a_send, r1_recv, r1_send, r2_recv, r2_send, rz2_recv, rz2_send, rz_recv, rz_send,
):
    me = lax.axis_index("ctx")
    x = me // NZ
    z = me % NZ
    xp = lax.rem(x + 1, NX)
    xm = lax.rem(x + NX - 1, NX)
    x2 = lax.rem(x + 2, NX)
    inner = (z == 1) | (z == 2)
    edge = (z == 0) | (z == 3)
    low = z < 2
    zi = jnp.where(low, z + 1, z - 1)
    zo = jnp.where(low, z - 1, z + 1)
    to = [xp * NZ + z, xm * NZ + z, x * NZ + zi, x * NZ + zo]
    zk = [z, jnp.where(lax.rem(z, 2) == 0, z + 1, z - 1), jnp.where(low, 2, 1), jnp.where(low, 3, 0)]
    column = {"A": x, "P": xp, "M": xm, "C": x2, "0": x, "p": xp, "m": xm, "2": x2}
    half = 8 * W // NB

    def owner_of(group, k):
        return column[group] * NZ + zk[k]

    def by_class(ends, middle):
        pl.when(edge)(ends)
        pl.when(inner)(middle)

    def pick(n, lo, hi, leaf):
        if hi - lo == 1:
            return leaf(lo)
        mid = (lo + hi) // 2
        return lax.cond(n < mid, lambda: pick(n, lo, mid, leaf), lambda: pick(n, mid, hi, leaf))

    def send(src, dst, ssem, rsem, dev):
        pltpu.make_async_remote_copy(
            src_ref=src, dst_ref=dst, send_sem=ssem, recv_sem=rsem, device_id={"ctx": dev}, device_id_type=MESH
        ).start()

    def wait_recv(dst, rsem):
        pltpu.make_async_remote_copy(
            src_ref=dst, dst_ref=dst, send_sem=rsem, recv_sem=rsem, device_id={"ctx": to[0]}, device_id_type=MESH
        ).wait_recv()

    def wait_send(ssem):
        pltpu.make_async_remote_copy(
            src_ref=G.at[0, 0], dst_ref=G.at[0, 0], send_sem=ssem, recv_sem=ssem, device_id={"ctx": to[0]},
            device_id_type=MESH,
        ).wait_send()

    own = [
        pltpu.make_async_copy(kc_hbm, G.at[me, :, 0], in_sem.at[0]),
        pltpu.make_async_copy(vc_hbm, G.at[me, :, 1], in_sem.at[1]),
    ]
    rest = [
        pltpu.make_async_copy(src, dst, in_sem.at[i + 2])
        for i, (src, dst) in enumerate(
            (
                (tk_hbm, tk_ref), (tv_hbm, tv_ref), (rl_hbm, rl_ref),
                (ro_hbm, ro_ref), (rt_hbm, rt_ref), (rs_hbm, rs_ref), (rc_hbm, rc_ref),
            )
        )
    ]
    rest += [
        pltpu.make_async_copy(src.at[:, pl.ds(i * W, W)], dst.at[i // 8, pl.ds(i % 8 * W, W)], q_sem.at[n, i])
        for i in range(16)
        for n, (src, dst) in enumerate(((q_hbm, QR), (do_hbm, DR)))
    ]
    for copy in own + rest:
        copy.start()

    barrier = pltpu.get_barrier_semaphore()

    def greet(dev):
        pl.semaphore_signal(barrier, inc=1, device_id={"ctx": dev}, device_id_type=MESH)

    for d in range(3):
        greet(to[d])
    pl.when(inner)(lambda: greet(to[3]))
    for copy in own:
        copy.wait()
    by_class(lambda: pl.semaphore_wait(barrier, 3), lambda: pl.semaphore_wait(barrier, 4))

    def gather_op(op):
        group, k, a = op[0], int(op[1]), int(op[2])
        owner = owner_of(group, k)
        tile = G.at[owner, a]
        if op[3] == "w":
            wait_recv(tile, a_recv.at[owner, a])
        else:
            d = int(op[3])
            send(tile, tile, a_send.at[d, 0 if group == "A" else 1, k, a], a_recv.at[owner, a], to[d])

    def gather_ops(cls, n):
        for op in GATHER[cls][n][0]:
            gather_op(op)

    by_class(lambda: gather_ops(0, 0), lambda: gather_ops(1, 0))

    for copy in rest:
        copy.wait()
    for h in range(2):
        for j in range(8):
            rows = slice(j * W, (j + 1) * W)
            QT[h, :, rows] = QR[h, rows, :].T
            DT[h, :, rows] = DR[h, rows, :].T
    reads = ro_ref.shape[1]
    tid = ro_ref[...] * 2 + rt_ref[...]
    live = lax.broadcasted_iota(jnp.int32, (1, reads), 1) < rc_ref[0]
    tid = jnp.where(live, tid, -1)
    named = lax.broadcasted_iota(jnp.int32, (2 * NX * NZ, reads), 0) == tid
    count0 = jnp.sum(jnp.where(named & (rs_ref[...] == 0), 1.0, 0.0), axis=1, keepdims=True)
    count1 = jnp.sum(jnp.where(named & (rs_ref[...] == 1), 1.0, 0.0), axis=1, keepdims=True)
    rl = rl_ref[...]
    times = jnp.where(rl == 0, count0, count1)
    bias_ref[...] = jnp.where(times > 0.5, jnp.log2(jnp.maximum(times, 1.0)), MASKED)
    cut = jnp.sum(jnp.where(rl == 0, 1.0, 0.0), axis=1, keepdims=True)
    key_at = lax.broadcasted_iota(jnp.int32, (W, W), 0)
    row_at = lax.broadcasted_iota(jnp.int32, (W, W), 1)
    tail_ok = (key_at <= row_at) & jnp.logical_not((key_at.astype(f32) < cut) & (row_at.astype(f32) >= cut))
    tail_ok = jnp.concatenate([tail_ok.astype(f32)] * (NB // W), axis=1) > 0.5

    for h in range(2):
        hs = slice(h * W, (h + 1) * W)
        for j in range(half):
            sl = slice(j * NB, (j + 1) * NB)
            s = jnp.dot(tk_ref[:, hs], QT[h, :, sl], preferred_element_type=f32)
            dp = jnp.dot(tv_ref[:, hs], DT[h, :, sl], preferred_element_type=f32)
            t = jnp.where(tail_ok, s * SCORE_TO_LOG2, MASKED).reshape(16, 8, NB)
            top = jnp.maximum(jnp.max(t, axis=0), FLOOR)
            e = jnp.exp2(t - top[None])
            low_sum = jnp.sum(e, axis=0)
            cross = jnp.sum(e * dp.reshape(16, 8, NB), axis=0)
            part = jnp.exp2(top - jnp.max(top, axis=0, keepdims=True))
            mean = jnp.sum(cross * part, axis=0, keepdims=True) / jnp.sum(low_sum * part, axis=0, keepdims=True)
            mean = jnp.broadcast_to(mean, (8, NB))
            m_ref[h, :, sl] = top
            l_ref[h, :, sl] = low_sum
            c_ref[h, :, sl] = cross - mean * low_sum
            shift_ref[h, :, sl] = mean

    def stats_tile(owner, a):
        b = jnp.broadcast_to(bias_ref[pl.ds(owner * 2 + a, 1), :], (8, W))
        b = jnp.concatenate([b] * (NB // W), axis=1)
        for h in range(2):
            hs = slice(h * W, (h + 1) * W)
            for j in range(half):
                sl = slice(j * NB, (j + 1) * NB)
                s = jnp.dot(G[owner, a, 0, :, hs], QT[h, :, sl], preferred_element_type=f32)
                dp = jnp.dot(G[owner, a, 1, :, hs], DT[h, :, sl], preferred_element_type=f32)
                t = (s * SCORE_TO_LOG2).reshape(16, 8, NB)
                old = m_ref[h, :, sl]
                new = jnp.maximum(old, jnp.max(t, axis=0) + b)
                fade = jnp.exp2(old - new)
                e = jnp.exp2(t - (new - b)[None])
                dlow = (dp.reshape(16, 8, NB) - shift_ref[h, :, sl][None]).astype(bf16)
                PS[owner, h, a, :, sl] = e.reshape(W, NB).astype(bf16)
                DS[owner, h, a, :, sl] = dlow.reshape(W, NB)
                top_ref[owner, a, h, :, sl] = new
                m_ref[h, :, sl] = new
                l_ref[h, :, sl] = l_ref[h, :, sl] * fade + jnp.sum(e, axis=0)
                c_ref[h, :, sl] = c_ref[h, :, sl] * fade + jnp.sum(e * dlow.astype(f32), axis=0)

    def gather_leaf(cls):
        def leaf(n):
            if n > 0:
                gather_ops(cls, n)
            op = GATHER[cls][n][1]
            return owner_of(op[0], int(op[1])) * 2 + int(op[2])

        return leaf

    def gather_step(n, carry):
        at = lax.cond(
            inner, lambda: pick(n, 0, 2 * NX * NZ, gather_leaf(1)), lambda: pick(n, 0, 2 * NX * NZ, gather_leaf(0))
        )
        stats_tile(at // 2, at % 2)
        return carry

    lax.fori_loop(0, 2 * NX * NZ, gather_step, 0)

    for h in range(2):
        m = m_ref[h]
        top = jnp.max(m, axis=0, keepdims=True)
        part = jnp.exp2(m - top)
        total = jnp.sum(l_ref[h] * part, axis=0, keepdims=True)
        cross = jnp.sum(c_ref[h] * part, axis=0, keepdims=True)
        m_ref[h] = jnp.broadcast_to(top + jnp.log2(total), (8, 8 * W))
        c_ref[h] = jnp.broadcast_to(cross / total, (8, 8 * W))
        dq_ref[h] = jnp.zeros((W, 8 * W), f32)

    def grads_chunk(owner):
        for h in range(2):
            hs = slice(h * W, (h + 1) * W)
            for a in range(2):
                for j in range(half):
                    sl = slice(j * NB, (j + 1) * NB)
                    f = jnp.exp2(top_ref[owner, a, h, :, sl] - m_ref[h, :, sl])
                    p = PS[owner, h, a, :, sl].astype(f32).reshape(16, 8, NB) * f[None]
                    d = p * (DS[owner, h, a, :, sl].astype(f32).reshape(16, 8, NB) - c_ref[h, :, sl][None])
                    PS[owner, h, a, :, sl] = p.reshape(W, NB).astype(bf16)
                    DS[owner, h, a, :, sl] = d.reshape(W, NB).astype(bf16)
            d_all = DS[owner, h].reshape(2 * W, 8 * W)
            keys = jnp.concatenate([G[owner, 0, 0, :, hs], G[owner, 1, 0, :, hs]], axis=0)
            dq_ref[h] += lax.dot_general(keys, d_all, TT, preferred_element_type=f32)
            dv = jnp.dot(PS[owner, h].reshape(2 * W, 8 * W), DR[h], preferred_element_type=f32)
            dk = jnp.dot(d_all, QR[h], preferred_element_type=f32) * SCALE
            for a in range(2):
                rows = slice(a * W, (a + 1) * W)
                GR[owner, a, 0, :, hs] = dk[rows].astype(bf16)
                GR[owner, a, 1, :, hs] = dv[rows].astype(bf16)

    def merge(ref, parts):
        def rows_of(i, carry):
            r = pl.ds(pl.multiple_of(i * 32, 32), 32)
            total = ref[:, r, :].astype(f32)
            for part in parts:
                total = total + part[:, r, :].astype(f32)
            ref[:, r, :] = total.astype(bf16)
            return carry

        lax.fori_loop(0, W // 32, rows_of, 0)

    def route(cls, group, k, a):
        needs = []
        if group == "2":
            if cls:
                needs.append((RZ2.at[k, a], rz2_recv.at[k, a]))
            if k >= 2:
                slot = k - 2 if cls else k
                return needs, 2, rz2_send.at[k - 2, a], RZ2.at[slot, a], rz2_recv.at[slot, a]
            return needs, 1 - a, r2_send.at[k, a], R2.at[k, a], r2_recv.at[k, a]
        if group in "mp":
            d = "mp".index(group)
            if k < 2 and a == d:
                needs.append((R2.at[k, a], r2_recv.at[k, a]))
            return needs, 1 - d, r1_send.at[d, k, a], R1.at[d, k, a], r1_recv.at[d, k, a]
        needs += [(R1.at[d, k, a], r1_recv.at[d, k, a]) for d in range(2)]
        if k == 0:
            needs += [(RZ.at[slot, a], rz_recv.at[slot, a]) for slot in ((0, 4) if cls else (0,))]
            return needs, None, None, None, None
        if cls:
            needs.append((RZ.at[k, a], rz_recv.at[k, a]))
            slot = 0 if k == 1 else k - 2
        else:
            slot = 4 if k == 1 else k
        return needs, 3 if cls and k == 1 else 2, rz_send.at[k - 1, a], RZ.at[slot, a], rz_recv.at[slot, a]

    def pass_on(cls, group, k, a):
        owner = owner_of(group, k)
        needs, d, ssem, there, rsem = route(cls, group, k, a)
        for ref, sem in needs:
            wait_recv(ref, sem)
        if d is None:
            rows = slice(a * W, (a + 1) * W)
            for i, out in enumerate((gck_ref, gcv_ref)):
                total = GR[owner, a, i].astype(f32)
                for ref, _ in needs:
                    total = total + ref[i].astype(f32)
                out[rows, :] = total
            return
        if needs:
            merge(GR.at[owner, a], [ref for ref, _ in needs])
        send(GR.at[owner, a], there, ssem, rsem, to[d])

    def after_chunk(cls, n):
        chunk, posts = SCATTER[cls][n]
        if chunk[0] not in "TU":
            for a in range(2):
                if not route(cls, chunk[0], int(chunk[1]), a)[0]:
                    pass_on(cls, chunk[0], int(chunk[1]), a)
        for post in posts:
            pass_on(cls, post[0], int(post[1]), int(post[2]))

    def chunk_leaf(cls):
        return lambda n: owner_of(SCATTER[cls][n][0][0], int(SCATTER[cls][n][0][1]))

    def after_leaf(cls):
        def leaf(n):
            after_chunk(cls, n)

        return leaf

    def scatter_step(n, carry):
        owner = lax.cond(
            inner, lambda: pick(n, 0, NX * NZ, chunk_leaf(1)), lambda: pick(n, 0, NX * NZ, chunk_leaf(0))
        )
        grads_chunk(owner)
        by_class(lambda: pick(n, 0, NX * NZ, after_leaf(0)), lambda: pick(n, 0, NX * NZ, after_leaf(1)))
        return carry

    lax.fori_loop(0, NX * NZ, scatter_step, 0)

    for h in range(2):
        hs = slice(h * W, (h + 1) * W)
        for j in range(half):
            sl = slice(j * NB, (j + 1) * NB)
            s = jnp.dot(tk_ref[:, hs], QT[h, :, sl], preferred_element_type=f32)
            dp = jnp.dot(tv_ref[:, hs], DT[h, :, sl], preferred_element_type=f32)
            t = jnp.where(tail_ok, s * SCORE_TO_LOG2, MASKED).reshape(16, 8, NB)
            p = jnp.exp2(t - m_ref[h, :, sl][None])
            d = p * (dp.reshape(16, 8, NB) - (c_ref[h, :, sl] + shift_ref[h, :, sl])[None])
            PS[0, h, 0, :, sl] = p.reshape(W, NB).astype(bf16)
            DS[0, h, 0, :, sl] = d.reshape(W, NB).astype(bf16)
        gv_ref[:, hs] = jnp.dot(PS[0, h, 0], DR[h], preferred_element_type=f32).astype(bf16)
        gk_ref[:, hs] = (jnp.dot(DS[0, h, 0], QR[h], preferred_element_type=f32) * SCALE).astype(bf16)
        dq_ref[h] += lax.dot_general(tk_ref[:, hs], DS[0, h, 0], TT, preferred_element_type=f32)
    by_class(lambda: after_chunk(0, NX * NZ), lambda: after_chunk(1, NX * NZ))
    for h in range(2):
        for j in range(8):
            gq_ref[:, (h * 8 + j) * W : (h * 8 + j + 1) * W] = (
                (dq_ref[h, :, j * W : (j + 1) * W] * SCALE).T.astype(bf16)
            )
    results = [
        pltpu.make_async_copy(src, dst, out_sem.at[i])
        for i, (src, dst) in enumerate(
            (
                (gq_ref, gq_hbm), (gk_ref, gk_hbm), (gv_ref, gv_hbm), (gck_ref, gck_hbm), (gcv_ref, gcv_hbm),
            )
        )
    ]
    for copy in results[:3]:
        copy.start()
    by_class(lambda: after_chunk(0, NX * NZ + 1), lambda: after_chunk(1, NX * NZ + 1))

    for copy in results[3:]:
        copy.start()

    def sums_left(cls):
        for group in "2mp0":
            for k in range(4):
                for a in range(2):
                    if group + str(k) != "00":
                        wait_send(route(cls, group, k, a)[2])

    def gather_left(cls):
        for ops, _ in GATHER[cls]:
            for op in ops:
                if op[3] != "w":
                    wait_send(a_send.at[int(op[3]), 0 if op[0] == "A" else 1, int(op[1]), int(op[2])])

    by_class(lambda: gather_left(0), lambda: gather_left(1))

    by_class(lambda: sums_left(0), lambda: sums_left(1))
    for copy in results:
        copy.wait()


def write_out(*refs):
    n = len(refs) // 2
    sem = refs[-1]
    copies = [pltpu.make_async_copy(refs[i], refs[n + i], sem.at[i]) for i in range(n)]
    for copy in copies:
        copy.start()
    for copy in copies:
        copy.wait()


def body(q, do, tk, tv, kc, vc, row_list, read_owner, read_tile, read_list, read_count):
    rows, width = q.shape
    kv_width = tk.shape[1]
    groups = width // kv_width
    reads = read_owner.shape[1]
    owners = NX * NZ
    hbm = pl.BlockSpec(memory_space=pltpu.HBM)
    tile = (2, W, kv_width)
    lanes = groups * W
    dma = pltpu.SemaphoreType.DMA
    scratch = [
        pltpu.VMEM((rows, width), bf16),
        pltpu.VMEM((rows, kv_width), bf16),
        pltpu.VMEM((rows, kv_width), bf16),
        pltpu.VMEM(kc.shape, f32),
        pltpu.VMEM(vc.shape, f32),
        pltpu.VMEM((rows, kv_width), bf16),
        pltpu.VMEM((rows, kv_width), bf16),
        pltpu.VMEM((1, rows), jnp.int32),
        pltpu.VMEM((1, reads), jnp.int32),
        pltpu.VMEM((1, reads), jnp.int32),
        pltpu.VMEM((1, reads), jnp.int32),
        pltpu.SMEM((1,), jnp.int32),
        pltpu.VMEM((owners, 2) + tile, bf16),
        pltpu.VMEM((owners, 2) + tile, bf16),
        pltpu.VMEM((2, 4, 2) + tile, bf16),
        pltpu.VMEM((2, 2) + tile, bf16),
        pltpu.VMEM((4, 2) + tile, bf16),
        pltpu.VMEM((5, 2) + tile, bf16),
        pltpu.VMEM((2, lanes, W), bf16),
        pltpu.VMEM((2, lanes, W), bf16),
        pltpu.VMEM((2, W, lanes), bf16),
        pltpu.VMEM((2, W, lanes), bf16),
        pltpu.VMEM((2, 8, lanes), f32),
        pltpu.VMEM((2, 8, lanes), f32),
        pltpu.VMEM((2, 8, lanes), f32),
        pltpu.VMEM((2, 8, lanes), f32),
        pltpu.VMEM((2 * owners, W), f32),
        pltpu.VMEM((2, W, lanes), f32),
        pltpu.VMEM((owners, 2, 2, W, lanes), bf16),
        pltpu.VMEM((owners, 2, 2, W, lanes), bf16),
        pltpu.VMEM((owners, 2, 2, 8, lanes), f32),
        dma((9,)),
        dma((2, 16)),
        dma((5,)),
        dma((owners, 2)),
        dma((4, 2, 4, 2)),
        dma((2, 4, 2)),
        dma((2, 4, 2)),
        dma((2, 2)),
        dma((2, 2)),
        dma((4, 2)),
        dma((2, 2)),
        dma((5, 2)),
        dma((3, 2)),
    ]
    pairs = 2 * groups * rows * (2 * owners + 1) * W * W * 2
    shapes = (
        jax.ShapeDtypeStruct((rows, width), bf16),
        jax.ShapeDtypeStruct((rows, kv_width), bf16),
        jax.ShapeDtypeStruct((rows, kv_width), bf16),
        jax.ShapeDtypeStruct(kc.shape, f32),
        jax.ShapeDtypeStruct(vc.shape, f32),
    )
    results = pl.pallas_call(
        kernel,
        name="tail_attention_backward",
        out_shape=shapes,
        in_specs=[hbm] * 11,
        out_specs=(hbm,) * 5,
        scratch_shapes=scratch,
        cost_estimate=pl.CostEstimate(flops=5 * pairs, bytes_accessed=4 << 20, transcendentals=pairs // W),
        compiler_params=pltpu.CompilerParams(collective_id=0, has_side_effects=True, vmem_limit_bytes=60 << 20),
    )(
        q, do, tk, tv, kc.reshape(2, W, kv_width), vc.reshape(2, W, kv_width),
        row_list.reshape(1, rows), read_owner, read_tile, read_list, read_count,
    )
    return pl.pallas_call(
        write_out,
        name="write_out",
        out_shape=shapes,
        in_specs=[pl.BlockSpec(memory_space=pltpu.VMEM)] * 5,
        out_specs=(hbm,) * 5,
        scratch_shapes=[dma((5,))],
        compiler_params=pltpu.CompilerParams(vmem_limit_bytes=60 << 20),
    )(*results)


def solution(mesh):
    split = P(("dp", "ctx"), "tp")
    per_ctx = P(("dp", "ctx"), None)
    flat = P(("dp", "ctx"))
    return jax.shard_map(
        body,
        mesh=mesh,
        in_specs=(split,) * 6 + (flat, per_ctx, per_ctx, per_ctx, flat),
        out_specs=(split,) * 5,
        check_vma=False,
    )
```

```python
import functools
import math

import jax
import jax.numpy as jnp
from jax import lax
from jax.experimental import pallas as pl
from jax.experimental.pallas import tpu as pltpu
from jax.sharding import PartitionSpec as P

W = 128
NX = 4
NZ = 4
SCALE = 1.0 / math.sqrt(W)
LOG2E = 1.4426950408889634
SCORE_TO_LOG2 = SCALE * LOG2E
MASKED = -1e30
FLOOR = -1e29
NB = 256
f32 = jnp.float32
bf16 = jnp.bfloat16
MESH = pl.DeviceIdType.MESH
TT = (((0,), (0,)), ((), ()))

GATHER = (
    (
        (("A000", "A001", "A002", "A010", "A011", "A012",), "A00"),
        ((), "A01"),
        (("A10w", "P00w", "M00w", "A100", "A101",), "A10"),
        ((), "P00"),
        ((), "M00"),
        (("A11w", "P01w", "M01w", "A110", "A111",), "A11"),
        ((), "P01"),
        ((), "M01"),
        (("A20w", "P10w", "M10w", "A200", "A201",), "A20"),
        ((), "P10"),
        ((), "M10"),
        (("A21w", "P11w", "M11w", "A210", "A211",), "A21"),
        ((), "P11"),
        ((), "M11"),
        (("A30w", "P20w", "M20w", "A300", "A301",), "A30"),
        ((), "P20"),
        ((), "M20"),
        (("A31w", "P21w", "M21w", "M000", "M100", "A310", "A311", "P011", "P111",), "A31"),
        ((), "P21"),
        ((), "M21"),
        (("C20w", "P30w", "M30w",), "C20"),
        ((), "P30"),
        ((), "M30"),
        (("C21w", "P31w", "M31w",), "C21"),
        ((), "P31"),
        ((), "M31"),
        (("C30w", "C00w", "C01w",), "C30"),
        ((), "C00"),
        ((), "C01"),
        (("C10w", "C31w", "C11w",), "C10"),
        ((), "C31"),
        ((), "C11"),
    ),
    (
        (("A002", "A000", "A001", "A003", "A012", "A010", "A011", "A013",), "A00"),
        ((), "A01"),
        (("A10w", "A20w", "P00w", "M00w", "A102", "M000", "A100", "A101", "A203",), "A10"),
        ((), "A20"),
        ((), "P00"),
        ((), "M00"),
        (("A11w", "A21w", "P01w", "M01w", "A201", "A112", "A110", "P011", "A111", "A213",), "A11"),
        ((), "A21"),
        ((), "P01"),
        ((), "M01"),
        (("A30w", "P10w", "C00w", "C002", "A303",), "A30"),
        ((), "P10"),
        ((), "C00"),
        (("M10w", "A31w", "C01w", "M100", "A200", "A300", "C012", "A210", "A310", "A313",), "M10"),
        ((), "A31"),
        ((), "C01"),
        (("C20w", "P11w", "M11w", "A301", "C203", "P111", "A211", "A311",), "C20"),
        ((), "P11"),
        ((), "M11"),
        (("P20w", "C10w", "C21w", "C102", "C213",), "P20"),
        ((), "C10"),
        ((), "C21"),
        (("M20w", "C11w", "C112",), "M20"),
        ((), "C11"),
        (("C30w", "C303",), "C30"),
        (("P21w", "M21w",), "P21"),
        ((), "M21"),
        (("C31w", "C313",), "C31"),
        (("P30w", "M30w",), "P30"),
        ((), "M30"),
        (("P31w", "M31w",), "P31"),
        ((), "M31"),
    ),
)
SCATTER = (
    (
        ("23", ()),
        ("m3", ()),
        ("21", ()),
        ("22", ()),
        ("p3", ()),
        ("p2", ()),
        ("m2", ()),
        ("p1", ("p11",)),
        ("01", ()),
        ("03", ("030",)),
        ("20", ()),
        ("m1", ("m10", "031",)),
        ("p0", ()),
        ("m0", ()),
        ("02", ("020",)),
        ("00", ()),
        ("T0", ("021",)),
        ("U0", ("m00", "011", "010", "p01", "000", "001",)),
    ),
    (
        ("m3", ()),
        ("p0", ()),
        ("p3", ()),
        ("m0", ()),
        ("23", ("230",)),
        ("21", ()),
        ("03", ()),
        ("01", ("231",)),
        ("p2", ("210",)),
        ("m1", ()),
        ("m2", ()),
        ("22", ("211", "220", "221",)),
        ("02", ("m10",)),
        ("p1", ()),
        ("20", ("030",)),
        ("00", ("200",)),
        ("T0", ("031",)),
        ("U0", ("p11", "201", "020", "021", "010", "011", "m00", "p01", "000", "001",)),
    ),
)


def kernel(
    q_hbm, do_hbm, tk_hbm, tv_hbm, kc_hbm, vc_hbm, rl_hbm, ro_hbm, rt_hbm, rs_hbm, rc_hbm,
    gq_ref, gk_ref, gv_ref, gck_ref, gcv_ref,
    tk_ref, tv_ref, rl_ref, ro_ref, rt_ref, rs_ref, rc_ref,
    G, GR, R1, R2, RZ2, RZ, QR, DR, QT, DT, m_ref, l_ref, c_ref, shift_ref, bias_ref, dq_ref, PS, DS, top_ref,
    in_sem, q_sem, a_recv, a_send, r1_recv, r1_send, r2_recv, r2_send, rz2_recv, rz2_send, rz_recv, rz_send,
):
    me = lax.axis_index("ctx")
    x = me // NZ
    z = me % NZ
    xp = lax.rem(x + 1, NX)
    xm = lax.rem(x + NX - 1, NX)
    x2 = lax.rem(x + 2, NX)
    inner = (z == 1) | (z == 2)
    edge = (z == 0) | (z == 3)
    low = z < 2
    zi = jnp.where(low, z + 1, z - 1)
    zo = jnp.where(low, z - 1, z + 1)
    to = [xp * NZ + z, xm * NZ + z, x * NZ + zi, x * NZ + zo]
    zk = [z, jnp.where(lax.rem(z, 2) == 0, z + 1, z - 1), jnp.where(low, 2, 1), jnp.where(low, 3, 0)]
    column = {"A": x, "P": xp, "M": xm, "C": x2, "0": x, "p": xp, "m": xm, "2": x2}
    half = 8 * W // NB

    def owner_of(group, k):
        return column[group] * NZ + zk[k]

    def by_class(ends, middle):
        pl.when(edge)(ends)
        pl.when(inner)(middle)

    def pick(n, lo, hi, leaf):
        if hi - lo == 1:
            return leaf(lo)
        mid = (lo + hi) // 2
        return lax.cond(n < mid, lambda: pick(n, lo, mid, leaf), lambda: pick(n, mid, hi, leaf))

    def send(src, dst, ssem, rsem, dev):
        pltpu.make_async_remote_copy(
            src_ref=src, dst_ref=dst, send_sem=ssem, recv_sem=rsem, device_id={"ctx": dev}, device_id_type=MESH
        ).start()

    def wait_recv(dst, rsem):
        pltpu.make_async_remote_copy(
            src_ref=dst, dst_ref=dst, send_sem=rsem, recv_sem=rsem, device_id={"ctx": to[0]}, device_id_type=MESH
        ).wait_recv()

    def wait_send(ssem):
        pltpu.make_async_remote_copy(
            src_ref=G.at[0, 0], dst_ref=G.at[0, 0], send_sem=ssem, recv_sem=ssem, device_id={"ctx": to[0]},
            device_id_type=MESH,
        ).wait_send()

    own = [
        pltpu.make_async_copy(kc_hbm, G.at[me, :, 0], in_sem.at[0]),
        pltpu.make_async_copy(vc_hbm, G.at[me, :, 1], in_sem.at[1]),
    ]
    rest = [
        pltpu.make_async_copy(src, dst, in_sem.at[i + 2])
        for i, (src, dst) in enumerate(
            (
                (tk_hbm, tk_ref), (tv_hbm, tv_ref), (rl_hbm, rl_ref),
                (ro_hbm, ro_ref), (rt_hbm, rt_ref), (rs_hbm, rs_ref), (rc_hbm, rc_ref),
            )
        )
    ]
    rest += [
        pltpu.make_async_copy(src.at[:, pl.ds(i * W, W)], dst.at[i // 8, pl.ds(i % 8 * W, W)], q_sem.at[n, i])
        for i in range(16)
        for n, (src, dst) in enumerate(((q_hbm, QR), (do_hbm, DR)))
    ]
    for copy in own + rest:
        copy.start()

    barrier = pltpu.get_barrier_semaphore()

    def greet(dev):
        pl.semaphore_signal(barrier, inc=1, device_id={"ctx": dev}, device_id_type=MESH)

    for d in range(3):
        greet(to[d])
    pl.when(inner)(lambda: greet(to[3]))
    for copy in own:
        copy.wait()
    by_class(lambda: pl.semaphore_wait(barrier, 3), lambda: pl.semaphore_wait(barrier, 4))

    def gather_op(op):
        group, k, a = op[0], int(op[1]), int(op[2])
        owner = owner_of(group, k)
        tile = G.at[owner, a]
        if op[3] == "w":
            wait_recv(tile, a_recv.at[owner, a])
        else:
            d = int(op[3])
            send(tile, tile, a_send.at[d, 0 if group == "A" else 1, k, a], a_recv.at[owner, a], to[d])

    def gather_ops(cls, n):
        for op in GATHER[cls][n][0]:
            gather_op(op)

    by_class(lambda: gather_ops(0, 0), lambda: gather_ops(1, 0))

    for copy in rest:
        copy.wait()
    for h in range(2):
        for j in range(8):
            rows = slice(j * W, (j + 1) * W)
            QT[h, :, rows] = QR[h, rows, :].T
            DT[h, :, rows] = DR[h, rows, :].T
    reads = ro_ref.shape[1]
    tid = ro_ref[...] * 2 + rt_ref[...]
    live = lax.broadcasted_iota(jnp.int32, (1, reads), 1) < rc_ref[0]
    tid = jnp.where(live, tid, -1)
    named = lax.broadcasted_iota(jnp.int32, (2 * NX * NZ, reads), 0) == tid
    count0 = jnp.sum(jnp.where(named & (rs_ref[...] == 0), 1.0, 0.0), axis=1, keepdims=True)
    count1 = jnp.sum(jnp.where(named & (rs_ref[...] == 1), 1.0, 0.0), axis=1, keepdims=True)
    rl = rl_ref[...]
    times = jnp.where(rl == 0, count0, count1)
    bias_ref[...] = jnp.where(times > 0.5, jnp.log2(jnp.maximum(times, 1.0)), MASKED)
    cut = jnp.sum(jnp.where(rl == 0, 1.0, 0.0), axis=1, keepdims=True)
    key_at = lax.broadcasted_iota(jnp.int32, (W, W), 0)
    row_at = lax.broadcasted_iota(jnp.int32, (W, W), 1)
    tail_ok = (key_at <= row_at) & jnp.logical_not((key_at.astype(f32) < cut) & (row_at.astype(f32) >= cut))
    tail_ok = jnp.concatenate([tail_ok.astype(f32)] * (NB // W), axis=1) > 0.5

    for h in range(2):
        hs = slice(h * W, (h + 1) * W)
        for j in range(half):
            sl = slice(j * NB, (j + 1) * NB)
            s = jnp.dot(tk_ref[:, hs], QT[h, :, sl], preferred_element_type=f32)
            dp = jnp.dot(tv_ref[:, hs], DT[h, :, sl], preferred_element_type=f32)
            t = jnp.where(tail_ok, s * SCORE_TO_LOG2, MASKED).reshape(16, 8, NB)
            top = jnp.maximum(jnp.max(t, axis=0), FLOOR)
            e = jnp.exp2(t - top[None])
            low_sum = jnp.sum(e, axis=0)
            cross = jnp.sum(e * dp.reshape(16, 8, NB), axis=0)
            part = jnp.exp2(top - jnp.max(top, axis=0, keepdims=True))
            mean = jnp.sum(cross * part, axis=0, keepdims=True) / jnp.sum(low_sum * part, axis=0, keepdims=True)
            mean = jnp.broadcast_to(mean, (8, NB))
            m_ref[h, :, sl] = top
            l_ref[h, :, sl] = low_sum
            c_ref[h, :, sl] = cross - mean * low_sum
            shift_ref[h, :, sl] = mean

    def stats_tile(owner, a):
        b = jnp.broadcast_to(bias_ref[pl.ds(owner * 2 + a, 1), :], (8, W))
        b = jnp.concatenate([b] * (NB // W), axis=1)
        for h in range(2):
            hs = slice(h * W, (h + 1) * W)
            for j in range(half):
                sl = slice(j * NB, (j + 1) * NB)
                s = jnp.dot(G[owner, a, 0, :, hs], QT[h, :, sl], preferred_element_type=f32)
                dp = jnp.dot(G[owner, a, 1, :, hs], DT[h, :, sl], preferred_element_type=f32)
                t = (s * SCORE_TO_LOG2).reshape(16, 8, NB)
                old = m_ref[h, :, sl]
                new = jnp.maximum(old, jnp.max(t, axis=0) + b)
                fade = jnp.exp2(old - new)
                e = jnp.exp2(t - (new - b)[None])
                dlow = (dp.reshape(16, 8, NB) - shift_ref[h, :, sl][None]).astype(bf16)
                PS[owner, h, a, :, sl] = e.reshape(W, NB).astype(bf16)
                DS[owner, h, a, :, sl] = dlow.reshape(W, NB)
                top_ref[owner, a, h, :, sl] = new
                m_ref[h, :, sl] = new
                l_ref[h, :, sl] = l_ref[h, :, sl] * fade + jnp.sum(e, axis=0)
                c_ref[h, :, sl] = c_ref[h, :, sl] * fade + jnp.sum(e * dlow.astype(f32), axis=0)

    def gather_leaf(cls):
        def leaf(n):
            if n > 0:
                gather_ops(cls, n)
            op = GATHER[cls][n][1]
            return owner_of(op[0], int(op[1])) * 2 + int(op[2])

        return leaf

    def gather_step(n, carry):
        at = lax.cond(
            inner, lambda: pick(n, 0, 2 * NX * NZ, gather_leaf(1)), lambda: pick(n, 0, 2 * NX * NZ, gather_leaf(0))
        )
        stats_tile(at // 2, at % 2)
        return carry

    lax.fori_loop(0, 2 * NX * NZ, gather_step, 0)

    for h in range(2):
        m = m_ref[h]
        top = jnp.max(m, axis=0, keepdims=True)
        part = jnp.exp2(m - top)
        total = jnp.sum(l_ref[h] * part, axis=0, keepdims=True)
        cross = jnp.sum(c_ref[h] * part, axis=0, keepdims=True)
        m_ref[h] = jnp.broadcast_to(top + jnp.log2(total), (8, 8 * W))
        c_ref[h] = jnp.broadcast_to(cross / total, (8, 8 * W))
        dq_ref[h] = jnp.zeros((W, 8 * W), f32)

    def grads_chunk(owner):
        for h in range(2):
            hs = slice(h * W, (h + 1) * W)
            for a in range(2):
                for j in range(half):
                    sl = slice(j * NB, (j + 1) * NB)
                    f = jnp.exp2(top_ref[owner, a, h, :, sl] - m_ref[h, :, sl])
                    p = PS[owner, h, a, :, sl].astype(f32).reshape(16, 8, NB) * f[None]
                    d = p * (DS[owner, h, a, :, sl].astype(f32).reshape(16, 8, NB) - c_ref[h, :, sl][None])
                    PS[owner, h, a, :, sl] = p.reshape(W, NB).astype(bf16)
                    DS[owner, h, a, :, sl] = d.reshape(W, NB).astype(bf16)
            d_all = DS[owner, h].reshape(2 * W, 8 * W)
            keys = jnp.concatenate([G[owner, 0, 0, :, hs], G[owner, 1, 0, :, hs]], axis=0)
            dq_ref[h] += lax.dot_general(keys, d_all, TT, preferred_element_type=f32)
            dv = jnp.dot(PS[owner, h].reshape(2 * W, 8 * W), DR[h], preferred_element_type=f32)
            dk = jnp.dot(d_all, QR[h], preferred_element_type=f32) * SCALE
            for a in range(2):
                rows = slice(a * W, (a + 1) * W)
                GR[owner, a, 0, :, hs] = dk[rows].astype(bf16)
                GR[owner, a, 1, :, hs] = dv[rows].astype(bf16)

    def merge(ref, parts):
        def rows_of(i, carry):
            r = pl.ds(pl.multiple_of(i * 32, 32), 32)
            total = ref[:, r, :].astype(f32)
            for part in parts:
                total = total + part[:, r, :].astype(f32)
            ref[:, r, :] = total.astype(bf16)
            return carry

        lax.fori_loop(0, W // 32, rows_of, 0)

    def route(cls, group, k, a):
        needs = []
        if group == "2":
            if cls:
                needs.append((RZ2.at[k, a], rz2_recv.at[k, a]))
            if k >= 2:
                slot = k - 2 if cls else k
                return needs, 2, rz2_send.at[k - 2, a], RZ2.at[slot, a], rz2_recv.at[slot, a]
            return needs, 1 - a, r2_send.at[k, a], R2.at[k, a], r2_recv.at[k, a]
        if group in "mp":
            d = "mp".index(group)
            if k < 2 and a == d:
                needs.append((R2.at[k, a], r2_recv.at[k, a]))
            return needs, 1 - d, r1_send.at[d, k, a], R1.at[d, k, a], r1_recv.at[d, k, a]
        needs += [(R1.at[d, k, a], r1_recv.at[d, k, a]) for d in range(2)]
        if k == 0:
            needs += [(RZ.at[slot, a], rz_recv.at[slot, a]) for slot in ((0, 4) if cls else (0,))]
            return needs, None, None, None, None
        if cls:
            needs.append((RZ.at[k, a], rz_recv.at[k, a]))
            slot = 0 if k == 1 else k - 2
        else:
            slot = 4 if k == 1 else k
        return needs, 3 if cls and k == 1 else 2, rz_send.at[k - 1, a], RZ.at[slot, a], rz_recv.at[slot, a]

    def pass_on(cls, group, k, a):
        owner = owner_of(group, k)
        needs, d, ssem, there, rsem = route(cls, group, k, a)
        for ref, sem in needs:
            wait_recv(ref, sem)
        if d is None:
            rows = slice(a * W, (a + 1) * W)
            for i, out in enumerate((gck_ref, gcv_ref)):
                total = GR[owner, a, i].astype(f32)
                for ref, _ in needs:
                    total = total + ref[i].astype(f32)
                out[rows, :] = total
            return
        if needs:
            merge(GR.at[owner, a], [ref for ref, _ in needs])
        send(GR.at[owner, a], there, ssem, rsem, to[d])

    def after_chunk(cls, n):
        chunk, posts = SCATTER[cls][n]
        if chunk[0] not in "TU":
            for a in range(2):
                if not route(cls, chunk[0], int(chunk[1]), a)[0]:
                    pass_on(cls, chunk[0], int(chunk[1]), a)
        for post in posts:
            pass_on(cls, post[0], int(post[1]), int(post[2]))

    def chunk_leaf(cls):
        return lambda n: owner_of(SCATTER[cls][n][0][0], int(SCATTER[cls][n][0][1]))

    def after_leaf(cls):
        def leaf(n):
            after_chunk(cls, n)

        return leaf

    def scatter_step(n, carry):
        owner = lax.cond(
            inner, lambda: pick(n, 0, NX * NZ, chunk_leaf(1)), lambda: pick(n, 0, NX * NZ, chunk_leaf(0))
        )
        grads_chunk(owner)
        by_class(lambda: pick(n, 0, NX * NZ, after_leaf(0)), lambda: pick(n, 0, NX * NZ, after_leaf(1)))
        return carry

    lax.fori_loop(0, NX * NZ, scatter_step, 0)

    for h in range(2):
        hs = slice(h * W, (h + 1) * W)
        for j in range(half):
            sl = slice(j * NB, (j + 1) * NB)
            s = jnp.dot(tk_ref[:, hs], QT[h, :, sl], preferred_element_type=f32)
            dp = jnp.dot(tv_ref[:, hs], DT[h, :, sl], preferred_element_type=f32)
            t = jnp.where(tail_ok, s * SCORE_TO_LOG2, MASKED).reshape(16, 8, NB)
            p = jnp.exp2(t - m_ref[h, :, sl][None])
            d = p * (dp.reshape(16, 8, NB) - (c_ref[h, :, sl] + shift_ref[h, :, sl])[None])
            PS[0, h, 0, :, sl] = p.reshape(W, NB).astype(bf16)
            DS[0, h, 0, :, sl] = d.reshape(W, NB).astype(bf16)
        gv_ref[:, hs] = jnp.dot(PS[0, h, 0], DR[h], preferred_element_type=f32).astype(bf16)
        gk_ref[:, hs] = (jnp.dot(DS[0, h, 0], QR[h], preferred_element_type=f32) * SCALE).astype(bf16)
        dq_ref[h] += lax.dot_general(tk_ref[:, hs], DS[0, h, 0], TT, preferred_element_type=f32)
    by_class(lambda: after_chunk(0, NX * NZ), lambda: after_chunk(1, NX * NZ))
    for h in range(2):
        for j in range(8):
            gq_ref[:, (h * 8 + j) * W : (h * 8 + j + 1) * W] = (
                (dq_ref[h, :, j * W : (j + 1) * W] * SCALE).T.astype(bf16)
            )
    by_class(lambda: after_chunk(0, NX * NZ + 1), lambda: after_chunk(1, NX * NZ + 1))

    def sums_left(cls):
        for group in "2mp0":
            for k in range(4):
                for a in range(2):
                    if group + str(k) != "00":
                        wait_send(route(cls, group, k, a)[2])

    def gather_left(cls):
        for ops, _ in GATHER[cls]:
            for op in ops:
                if op[3] != "w":
                    wait_send(a_send.at[int(op[3]), 0 if op[0] == "A" else 1, int(op[1]), int(op[2])])

    by_class(lambda: gather_left(0), lambda: gather_left(1))

    by_class(lambda: sums_left(0), lambda: sums_left(1))


def write_out(*refs):
    n = len(refs) // 2
    sem = refs[-1]
    copies = [pltpu.make_async_copy(refs[i], refs[n + i], sem.at[i]) for i in range(n)]
    for copy in copies:
        copy.start()
    for copy in copies:
        copy.wait()


def body(q, do, tk, tv, kc, vc, row_list, read_owner, read_tile, read_list, read_count):
    rows, width = q.shape
    kv_width = tk.shape[1]
    groups = width // kv_width
    reads = read_owner.shape[1]
    owners = NX * NZ
    vmem = pl.BlockSpec(memory_space=pltpu.VMEM)
    hbm = pl.BlockSpec(memory_space=pl.ANY)
    tile = (2, W, kv_width)
    lanes = groups * W
    dma = pltpu.SemaphoreType.DMA
    scratch = [
        pltpu.VMEM((rows, kv_width), bf16),
        pltpu.VMEM((rows, kv_width), bf16),
        pltpu.VMEM((1, rows), jnp.int32),
        pltpu.VMEM((1, reads), jnp.int32),
        pltpu.VMEM((1, reads), jnp.int32),
        pltpu.VMEM((1, reads), jnp.int32),
        pltpu.SMEM((1,), jnp.int32),
        pltpu.VMEM((owners, 2) + tile, bf16),
        pltpu.VMEM((owners, 2) + tile, bf16),
        pltpu.VMEM((2, 4, 2) + tile, bf16),
        pltpu.VMEM((2, 2) + tile, bf16),
        pltpu.VMEM((4, 2) + tile, bf16),
        pltpu.VMEM((5, 2) + tile, bf16),
        pltpu.VMEM((2, lanes, W), bf16),
        pltpu.VMEM((2, lanes, W), bf16),
        pltpu.VMEM((2, W, lanes), bf16),
        pltpu.VMEM((2, W, lanes), bf16),
        pltpu.VMEM((2, 8, lanes), f32),
        pltpu.VMEM((2, 8, lanes), f32),
        pltpu.VMEM((2, 8, lanes), f32),
        pltpu.VMEM((2, 8, lanes), f32),
        pltpu.VMEM((2 * owners, W), f32),
        pltpu.VMEM((2, W, lanes), f32),
        pltpu.VMEM((owners, 2, 2, W, lanes), bf16),
        pltpu.VMEM((owners, 2, 2, W, lanes), bf16),
        pltpu.VMEM((owners, 2, 2, 8, lanes), f32),
        dma((9,)),
        dma((2, 16)),
        dma((owners, 2)),
        dma((4, 2, 4, 2)),
        dma((2, 4, 2)),
        dma((2, 4, 2)),
        dma((2, 2)),
        dma((2, 2)),
        dma((4, 2)),
        dma((2, 2)),
        dma((5, 2)),
        dma((3, 2)),
    ]
    pairs = 2 * groups * rows * (2 * owners + 1) * W * W * 2
    shapes = (
        jax.ShapeDtypeStruct((rows, width), bf16),
        jax.ShapeDtypeStruct((rows, kv_width), bf16),
        jax.ShapeDtypeStruct((rows, kv_width), bf16),
        jax.ShapeDtypeStruct(kc.shape, f32),
        jax.ShapeDtypeStruct(vc.shape, f32),
    )
    results = pl.pallas_call(
        kernel,
        name="tail_attention_backward",
        out_shape=shapes,
        in_specs=[hbm] * 11,
        out_specs=(vmem,) * 5,
        scratch_shapes=scratch,
        cost_estimate=pl.CostEstimate(flops=5 * pairs, bytes_accessed=4 << 20, transcendentals=pairs // W),
        compiler_params=pltpu.CompilerParams(collective_id=0, has_side_effects=True, vmem_limit_bytes=60 << 20),
    )(
        q, do, tk, tv, kc.reshape(2, W, kv_width), vc.reshape(2, W, kv_width),
        row_list.reshape(1, rows), read_owner, read_tile, read_list, read_count,
    )
    return pl.pallas_call(
        write_out,
        name="write_out",
        out_shape=shapes,
        in_specs=[vmem] * 5,
        out_specs=(hbm,) * 5,
        scratch_shapes=[dma((5,))],
        compiler_params=pltpu.CompilerParams(vmem_limit_bytes=60 << 20),
    )(*results)


def solution(mesh):
    split = P(("dp", "ctx"), "tp")
    per_ctx = P(("dp", "ctx"), None)
    flat = P(("dp", "ctx"))
    return jax.shard_map(
        body,
        mesh=mesh,
        in_specs=(split,) * 6 + (flat, per_ctx, per_ctx, per_ctx, flat),
        out_specs=(split,) * 5,
        check_vma=False,
    )
```

```python
import functools
import math

import jax
import jax.numpy as jnp
from jax import lax
from jax.experimental import pallas as pl
from jax.experimental.pallas import tpu as pltpu
from jax.sharding import PartitionSpec as P

W = 128
NX = 4
NZ = 4
SCALE = 1.0 / math.sqrt(W)
LOG2E = 1.4426950408889634
SCORE_TO_LOG2 = SCALE * LOG2E
MASKED = -1e30
FLOOR = -1e29
NB = 256
f32 = jnp.float32
bf16 = jnp.bfloat16
MESH = pl.DeviceIdType.MESH
TT = (((0,), (0,)), ((), ()))

GATHER = (
    (
        (("A000", "A001", "A002", "A010", "A011", "A012",), "A00"),
        ((), "A01"),
        (("A10w", "P00w", "M00w", "A100", "A101",), "A10"),
        ((), "P00"),
        ((), "M00"),
        (("A11w", "P01w", "M01w", "A110", "A111",), "A11"),
        ((), "P01"),
        ((), "M01"),
        (("A20w", "P10w", "M10w", "A200", "A201",), "A20"),
        ((), "P10"),
        ((), "M10"),
        (("A21w", "P11w", "M11w", "A210", "A211",), "A21"),
        ((), "P11"),
        ((), "M11"),
        (("A30w", "P20w", "M20w", "A300", "A301",), "A30"),
        ((), "P20"),
        ((), "M20"),
        (("A31w", "P21w", "M21w", "M000", "M100", "A310", "A311", "P011", "P111",), "A31"),
        ((), "P21"),
        ((), "M21"),
        (("C20w", "P30w", "M30w",), "C20"),
        ((), "P30"),
        ((), "M30"),
        (("C21w", "P31w", "M31w",), "C21"),
        ((), "P31"),
        ((), "M31"),
        (("C30w", "C00w", "C01w",), "C30"),
        ((), "C00"),
        ((), "C01"),
        (("C10w", "C31w", "C11w",), "C10"),
        ((), "C31"),
        ((), "C11"),
    ),
    (
        (("A002", "A000", "A001", "A003", "A012", "A010", "A011", "A013",), "A00"),
        ((), "A01"),
        (("A10w", "A20w", "P00w", "M00w", "A102", "M000", "A100", "A101", "A203",), "A10"),
        ((), "A20"),
        ((), "P00"),
        ((), "M00"),
        (("A11w", "A21w", "P01w", "M01w", "A201", "A112", "A110", "P011", "A111", "A213",), "A11"),
        ((), "A21"),
        ((), "P01"),
        ((), "M01"),
        (("A30w", "P10w", "C00w", "C002", "A303",), "A30"),
        ((), "P10"),
        ((), "C00"),
        (("M10w", "A31w", "C01w", "M100", "A200", "A300", "C012", "A210", "A310", "A313",), "M10"),
        ((), "A31"),
        ((), "C01"),
        (("C20w", "P11w", "M11w", "A301", "C203", "P111", "A211", "A311",), "C20"),
        ((), "P11"),
        ((), "M11"),
        (("P20w", "C10w", "C21w", "C102", "C213",), "P20"),
        ((), "C10"),
        ((), "C21"),
        (("M20w", "C11w", "C112",), "M20"),
        ((), "C11"),
        (("C30w", "C303",), "C30"),
        (("P21w", "M21w",), "P21"),
        ((), "M21"),
        (("C31w", "C313",), "C31"),
        (("P30w", "M30w",), "P30"),
        ((), "M30"),
        (("P31w", "M31w",), "P31"),
        ((), "M31"),
    ),
)
SCATTER = (
    (
        ("23", ()),
        ("m3", ()),
        ("21", ()),
        ("22", ()),
        ("p3", ()),
        ("p2", ()),
        ("m2", ()),
        ("p1", ("p11",)),
        ("01", ()),
        ("03", ("030",)),
        ("20", ()),
        ("m1", ("m10", "031",)),
        ("p0", ()),
        ("m0", ()),
        ("02", ("020",)),
        ("00", ()),
        ("T0", ("021",)),
        ("U0", ("m00", "011", "010", "p01", "000", "001",)),
    ),
    (
        ("m3", ()),
        ("p0", ()),
        ("p3", ()),
        ("m0", ()),
        ("23", ("230",)),
        ("21", ()),
        ("03", ()),
        ("01", ("231",)),
        ("p2", ("210",)),
        ("m1", ()),
        ("m2", ()),
        ("22", ("211", "220", "221",)),
        ("02", ("m10",)),
        ("p1", ()),
        ("20", ("030",)),
        ("00", ("200",)),
        ("T0", ("031",)),
        ("U0", ("p11", "201", "020", "021", "010", "011", "m00", "p01", "000", "001",)),
    ),
)


def kernel(
    q_hbm, do_hbm, tk_hbm, tv_hbm, kc_hbm, vc_hbm, rl_hbm, ro_hbm, rt_hbm, rs_hbm, rc_hbm,
    gq_ref, gk_ref, gv_ref, gck_ref, gcv_ref,
    tk_ref, tv_ref, rl_ref, ro_ref, rt_ref, rs_ref, rc_ref,
    G, R1, R2, RZ2, RZ, QR, DR, QT, DT, m_ref, l_ref, c_ref, shift_ref, bias_ref, dq_ref, PS, DS, top_ref,
    in_sem, q_sem, a_recv, a_send, r1_recv, r1_send, r2_recv, r2_send, rz2_recv, rz2_send, rz_recv, rz_send,
):
    me = lax.axis_index("ctx")
    x = me // NZ
    z = me % NZ
    xp = lax.rem(x + 1, NX)
    xm = lax.rem(x + NX - 1, NX)
    x2 = lax.rem(x + 2, NX)
    inner = (z == 1) | (z == 2)
    edge = (z == 0) | (z == 3)
    low = z < 2
    zi = jnp.where(low, z + 1, z - 1)
    zo = jnp.where(low, z - 1, z + 1)
    to = [xp * NZ + z, xm * NZ + z, x * NZ + zi, x * NZ + zo]
    zk = [z, jnp.where(lax.rem(z, 2) == 0, z + 1, z - 1), jnp.where(low, 2, 1), jnp.where(low, 3, 0)]
    column = {"A": x, "P": xp, "M": xm, "C": x2, "0": x, "p": xp, "m": xm, "2": x2}
    half = 8 * W // NB

    def owner_of(group, k):
        return column[group] * NZ + zk[k]

    def by_class(ends, middle):
        pl.when(edge)(ends)
        pl.when(inner)(middle)

    def pick(n, lo, hi, leaf):
        if hi - lo == 1:
            return leaf(lo)
        mid = (lo + hi) // 2
        return lax.cond(n < mid, lambda: pick(n, lo, mid, leaf), lambda: pick(n, mid, hi, leaf))

    def send(src, dst, ssem, rsem, dev):
        pltpu.make_async_remote_copy(
            src_ref=src, dst_ref=dst, send_sem=ssem, recv_sem=rsem, device_id={"ctx": dev}, device_id_type=MESH
        ).start()

    def wait_recv(dst, rsem):
        pltpu.make_async_remote_copy(
            src_ref=dst, dst_ref=dst, send_sem=rsem, recv_sem=rsem, device_id={"ctx": to[0]}, device_id_type=MESH
        ).wait_recv()

    def wait_send(ssem):
        pltpu.make_async_remote_copy(
            src_ref=G.at[0, 0], dst_ref=G.at[0, 0], send_sem=ssem, recv_sem=ssem, device_id={"ctx": to[0]},
            device_id_type=MESH,
        ).wait_send()

    own = [
        pltpu.make_async_copy(kc_hbm, G.at[me, :, 0], in_sem.at[0]),
        pltpu.make_async_copy(vc_hbm, G.at[me, :, 1], in_sem.at[1]),
    ]
    rest = [
        pltpu.make_async_copy(src, dst, in_sem.at[i + 2])
        for i, (src, dst) in enumerate(
            (
                (tk_hbm, tk_ref), (tv_hbm, tv_ref), (rl_hbm, rl_ref),
                (ro_hbm, ro_ref), (rt_hbm, rt_ref), (rs_hbm, rs_ref), (rc_hbm, rc_ref),
            )
        )
    ]
    rest += [
        pltpu.make_async_copy(src.at[:, pl.ds(i * W, W)], dst.at[i // 8, pl.ds(i % 8 * W, W)], q_sem.at[n, i])
        for i in range(16)
        for n, (src, dst) in enumerate(((q_hbm, QR), (do_hbm, DR)))
    ]
    for copy in own + rest:
        copy.start()

    barrier = pltpu.get_barrier_semaphore()

    def greet(dev):
        pl.semaphore_signal(barrier, inc=1, device_id={"ctx": dev}, device_id_type=MESH)

    for d in range(3):
        greet(to[d])
    pl.when(inner)(lambda: greet(to[3]))
    for copy in own:
        copy.wait()
    by_class(lambda: pl.semaphore_wait(barrier, 3), lambda: pl.semaphore_wait(barrier, 4))

    def gather_op(op):
        group, k, a = op[0], int(op[1]), int(op[2])
        owner = owner_of(group, k)
        tile = G.at[owner, a]
        if op[3] == "w":
            wait_recv(tile, a_recv.at[owner, a])
        else:
            d = int(op[3])
            send(tile, tile, a_send.at[d, 0 if group == "A" else 1, k, a], a_recv.at[owner, a], to[d])

    def gather_ops(cls, n):
        for op in GATHER[cls][n][0]:
            gather_op(op)

    by_class(lambda: gather_ops(0, 0), lambda: gather_ops(1, 0))

    for copy in rest:
        copy.wait()
    for h in range(2):
        for j in range(8):
            rows = slice(j * W, (j + 1) * W)
            QT[h, :, rows] = QR[h, rows, :].T
            DT[h, :, rows] = DR[h, rows, :].T
    reads = ro_ref.shape[1]
    tid = ro_ref[...] * 2 + rt_ref[...]
    live = lax.broadcasted_iota(jnp.int32, (1, reads), 1) < rc_ref[0]
    tid = jnp.where(live, tid, -1)
    named = lax.broadcasted_iota(jnp.int32, (2 * NX * NZ, reads), 0) == tid
    count0 = jnp.sum(jnp.where(named & (rs_ref[...] == 0), 1.0, 0.0), axis=1, keepdims=True)
    count1 = jnp.sum(jnp.where(named & (rs_ref[...] == 1), 1.0, 0.0), axis=1, keepdims=True)
    rl = rl_ref[...]
    times = jnp.where(rl == 0, count0, count1)
    bias_ref[...] = jnp.where(times > 0.5, jnp.log2(jnp.maximum(times, 1.0)), MASKED)
    cut = jnp.sum(jnp.where(rl == 0, 1.0, 0.0), axis=1, keepdims=True)
    key_at = lax.broadcasted_iota(jnp.int32, (W, W), 0)
    row_at = lax.broadcasted_iota(jnp.int32, (W, W), 1)
    tail_ok = (key_at <= row_at) & jnp.logical_not((key_at.astype(f32) < cut) & (row_at.astype(f32) >= cut))
    tail_ok = jnp.concatenate([tail_ok.astype(f32)] * (NB // W), axis=1) > 0.5

    for h in range(2):
        hs = slice(h * W, (h + 1) * W)
        for j in range(half):
            sl = slice(j * NB, (j + 1) * NB)
            s = jnp.dot(tk_ref[:, hs], QT[h, :, sl], preferred_element_type=f32)
            dp = jnp.dot(tv_ref[:, hs], DT[h, :, sl], preferred_element_type=f32)
            t = jnp.where(tail_ok, s * SCORE_TO_LOG2, MASKED).reshape(16, 8, NB)
            top = jnp.maximum(jnp.max(t, axis=0), FLOOR)
            e = jnp.exp2(t - top[None])
            low_sum = jnp.sum(e, axis=0)
            cross = jnp.sum(e * dp.reshape(16, 8, NB), axis=0)
            part = jnp.exp2(top - jnp.max(top, axis=0, keepdims=True))
            mean = jnp.sum(cross * part, axis=0, keepdims=True) / jnp.sum(low_sum * part, axis=0, keepdims=True)
            mean = jnp.broadcast_to(mean, (8, NB))
            m_ref[h, :, sl] = top
            l_ref[h, :, sl] = low_sum
            c_ref[h, :, sl] = cross - mean * low_sum
            shift_ref[h, :, sl] = mean

    def stats_tile(owner, a):
        b = jnp.broadcast_to(bias_ref[pl.ds(owner * 2 + a, 1), :], (8, W))
        b = jnp.concatenate([b] * (NB // W), axis=1)
        for h in range(2):
            hs = slice(h * W, (h + 1) * W)
            for j in range(half):
                sl = slice(j * NB, (j + 1) * NB)
                s = jnp.dot(G[owner, a, 0, :, hs], QT[h, :, sl], preferred_element_type=f32)
                dp = jnp.dot(G[owner, a, 1, :, hs], DT[h, :, sl], preferred_element_type=f32)
                t = (s * SCORE_TO_LOG2).reshape(16, 8, NB)
                old = m_ref[h, :, sl]
                new = jnp.maximum(old, jnp.max(t, axis=0) + b)
                fade = jnp.exp2(old - new)
                e = jnp.exp2(t - (new - b)[None])
                dlow = (dp.reshape(16, 8, NB) - shift_ref[h, :, sl][None]).astype(bf16)
                PS[owner, h, a, :, sl] = e.reshape(W, NB).astype(bf16)
                DS[owner, h, a, :, sl] = dlow.reshape(W, NB)
                top_ref[owner, a, h, :, sl] = new
                m_ref[h, :, sl] = new
                l_ref[h, :, sl] = l_ref[h, :, sl] * fade + jnp.sum(e, axis=0)
                c_ref[h, :, sl] = c_ref[h, :, sl] * fade + jnp.sum(e * dlow.astype(f32), axis=0)

    def gather_leaf(cls):
        def leaf(n):
            if n > 0:
                gather_ops(cls, n)
            op = GATHER[cls][n][1]
            return owner_of(op[0], int(op[1])) * 2 + int(op[2])

        return leaf

    def gather_step(n, carry):
        at = lax.cond(
            inner, lambda: pick(n, 0, 2 * NX * NZ, gather_leaf(1)), lambda: pick(n, 0, 2 * NX * NZ, gather_leaf(0))
        )
        stats_tile(at // 2, at % 2)
        return carry

    lax.fori_loop(0, 2 * NX * NZ, gather_step, 0)

    for h in range(2):
        m = m_ref[h]
        top = jnp.max(m, axis=0, keepdims=True)
        part = jnp.exp2(m - top)
        total = jnp.sum(l_ref[h] * part, axis=0, keepdims=True)
        cross = jnp.sum(c_ref[h] * part, axis=0, keepdims=True)
        m_ref[h] = jnp.broadcast_to(top + jnp.log2(total), (8, 8 * W))
        c_ref[h] = jnp.broadcast_to(cross / total, (8, 8 * W))
        dq_ref[h] = jnp.zeros((W, 8 * W), f32)

    def gather_left(cls):
        for ops, _ in GATHER[cls]:
            for op in ops:
                if op[3] != "w":
                    wait_send(a_send.at[int(op[3]), 0 if op[0] == "A" else 1, int(op[1]), int(op[2])])

    by_class(lambda: gather_left(0), lambda: gather_left(1))

    def grads_chunk(owner):
        for h in range(2):
            hs = slice(h * W, (h + 1) * W)
            for a in range(2):
                for j in range(half):
                    sl = slice(j * NB, (j + 1) * NB)
                    f = jnp.exp2(top_ref[owner, a, h, :, sl] - m_ref[h, :, sl])
                    p = PS[owner, h, a, :, sl].astype(f32).reshape(16, 8, NB) * f[None]
                    d = p * (DS[owner, h, a, :, sl].astype(f32).reshape(16, 8, NB) - c_ref[h, :, sl][None])
                    PS[owner, h, a, :, sl] = p.reshape(W, NB).astype(bf16)
                    DS[owner, h, a, :, sl] = d.reshape(W, NB).astype(bf16)
            d_all = DS[owner, h].reshape(2 * W, 8 * W)
            keys = jnp.concatenate([G[owner, 0, 0, :, hs], G[owner, 1, 0, :, hs]], axis=0)
            dq_ref[h] += lax.dot_general(keys, d_all, TT, preferred_element_type=f32)
            dv = jnp.dot(PS[owner, h].reshape(2 * W, 8 * W), DR[h], preferred_element_type=f32)
            dk = jnp.dot(d_all, QR[h], preferred_element_type=f32) * SCALE
            for a in range(2):
                rows = slice(a * W, (a + 1) * W)
                G[owner, a, 0, :, hs] = dk[rows].astype(bf16)
                G[owner, a, 1, :, hs] = dv[rows].astype(bf16)

    def merge(ref, parts):
        def rows_of(i, carry):
            r = pl.ds(pl.multiple_of(i * 32, 32), 32)
            total = ref[:, r, :].astype(f32)
            for part in parts:
                total = total + part[:, r, :].astype(f32)
            ref[:, r, :] = total.astype(bf16)
            return carry

        lax.fori_loop(0, W // 32, rows_of, 0)

    def route(cls, group, k, a):
        needs = []
        if group == "2":
            if cls:
                needs.append((RZ2.at[k, a], rz2_recv.at[k, a]))
            if k >= 2:
                slot = k - 2 if cls else k
                return needs, 2, rz2_send.at[k - 2, a], RZ2.at[slot, a], rz2_recv.at[slot, a]
            return needs, 1 - a, r2_send.at[k, a], R2.at[k, a], r2_recv.at[k, a]
        if group in "mp":
            d = "mp".index(group)
            if k < 2 and a == d:
                needs.append((R2.at[k, a], r2_recv.at[k, a]))
            return needs, 1 - d, r1_send.at[d, k, a], R1.at[d, k, a], r1_recv.at[d, k, a]
        needs += [(R1.at[d, k, a], r1_recv.at[d, k, a]) for d in range(2)]
        if k == 0:
            needs += [(RZ.at[slot, a], rz_recv.at[slot, a]) for slot in ((0, 4) if cls else (0,))]
            return needs, None, None, None, None
        if cls:
            needs.append((RZ.at[k, a], rz_recv.at[k, a]))
            slot = 0 if k == 1 else k - 2
        else:
            slot = 4 if k == 1 else k
        return needs, 3 if cls and k == 1 else 2, rz_send.at[k - 1, a], RZ.at[slot, a], rz_recv.at[slot, a]

    def pass_on(cls, group, k, a):
        owner = owner_of(group, k)
        needs, d, ssem, there, rsem = route(cls, group, k, a)
        for ref, sem in needs:
            wait_recv(ref, sem)
        if d is None:
            rows = slice(a * W, (a + 1) * W)
            for i, out in enumerate((gck_ref, gcv_ref)):
                total = G[owner, a, i].astype(f32)
                for ref, _ in needs:
                    total = total + ref[i].astype(f32)
                out[rows, :] = total
            return
        if needs:
            merge(G.at[owner, a], [ref for ref, _ in needs])
        send(G.at[owner, a], there, ssem, rsem, to[d])

    def after_chunk(cls, n):
        chunk, posts = SCATTER[cls][n]
        if chunk[0] not in "TU":
            for a in range(2):
                if not route(cls, chunk[0], int(chunk[1]), a)[0]:
                    pass_on(cls, chunk[0], int(chunk[1]), a)
        for post in posts:
            pass_on(cls, post[0], int(post[1]), int(post[2]))

    def chunk_leaf(cls):
        return lambda n: owner_of(SCATTER[cls][n][0][0], int(SCATTER[cls][n][0][1]))

    def after_leaf(cls):
        def leaf(n):
            after_chunk(cls, n)

        return leaf

    def scatter_step(n, carry):
        owner = lax.cond(
            inner, lambda: pick(n, 0, NX * NZ, chunk_leaf(1)), lambda: pick(n, 0, NX * NZ, chunk_leaf(0))
        )
        grads_chunk(owner)
        by_class(lambda: pick(n, 0, NX * NZ, after_leaf(0)), lambda: pick(n, 0, NX * NZ, after_leaf(1)))
        return carry

    lax.fori_loop(0, NX * NZ, scatter_step, 0)

    for h in range(2):
        hs = slice(h * W, (h + 1) * W)
        for j in range(half):
            sl = slice(j * NB, (j + 1) * NB)
            s = jnp.dot(tk_ref[:, hs], QT[h, :, sl], preferred_element_type=f32)
            dp = jnp.dot(tv_ref[:, hs], DT[h, :, sl], preferred_element_type=f32)
            t = jnp.where(tail_ok, s * SCORE_TO_LOG2, MASKED).reshape(16, 8, NB)
            p = jnp.exp2(t - m_ref[h, :, sl][None])
            d = p * (dp.reshape(16, 8, NB) - (c_ref[h, :, sl] + shift_ref[h, :, sl])[None])
            PS[0, h, 0, :, sl] = p.reshape(W, NB).astype(bf16)
            DS[0, h, 0, :, sl] = d.reshape(W, NB).astype(bf16)
        gv_ref[:, hs] = jnp.dot(PS[0, h, 0], DR[h], preferred_element_type=f32).astype(bf16)
        gk_ref[:, hs] = (jnp.dot(DS[0, h, 0], QR[h], preferred_element_type=f32) * SCALE).astype(bf16)
        dq_ref[h] += lax.dot_general(tk_ref[:, hs], DS[0, h, 0], TT, preferred_element_type=f32)
    by_class(lambda: after_chunk(0, NX * NZ), lambda: after_chunk(1, NX * NZ))
    for h in range(2):
        for j in range(8):
            gq_ref[:, (h * 8 + j) * W : (h * 8 + j + 1) * W] = (
                (dq_ref[h, :, j * W : (j + 1) * W] * SCALE).T.astype(bf16)
            )
    by_class(lambda: after_chunk(0, NX * NZ + 1), lambda: after_chunk(1, NX * NZ + 1))

    def sums_left(cls):
        for group in "2mp0":
            for k in range(4):
                for a in range(2):
                    if group + str(k) != "00":
                        wait_send(route(cls, group, k, a)[2])


    by_class(lambda: sums_left(0), lambda: sums_left(1))


def write_out(*refs):
    n = len(refs) // 2
    sem = refs[-1]
    copies = [pltpu.make_async_copy(refs[i], refs[n + i], sem.at[i]) for i in range(n)]
    for copy in copies:
        copy.start()
    for copy in copies:
        copy.wait()


def body(q, do, tk, tv, kc, vc, row_list, read_owner, read_tile, read_list, read_count):
    rows, width = q.shape
    kv_width = tk.shape[1]
    groups = width // kv_width
    reads = read_owner.shape[1]
    owners = NX * NZ
    vmem = pl.BlockSpec(memory_space=pltpu.VMEM)
    hbm = pl.BlockSpec(memory_space=pl.ANY)
    tile = (2, W, kv_width)
    lanes = groups * W
    dma = pltpu.SemaphoreType.DMA
    scratch = [
        pltpu.VMEM((rows, kv_width), bf16),
        pltpu.VMEM((rows, kv_width), bf16),
        pltpu.VMEM((1, rows), jnp.int32),
        pltpu.VMEM((1, reads), jnp.int32),
        pltpu.VMEM((1, reads), jnp.int32),
        pltpu.VMEM((1, reads), jnp.int32),
        pltpu.SMEM((1,), jnp.int32),
        pltpu.VMEM((owners, 2) + tile, bf16),
        pltpu.VMEM((2, 4, 2) + tile, bf16),
        pltpu.VMEM((2, 2) + tile, bf16),
        pltpu.VMEM((4, 2) + tile, bf16),
        pltpu.VMEM((5, 2) + tile, bf16),
        pltpu.VMEM((2, lanes, W), bf16),
        pltpu.VMEM((2, lanes, W), bf16),
        pltpu.VMEM((2, W, lanes), bf16),
        pltpu.VMEM((2, W, lanes), bf16),
        pltpu.VMEM((2, 8, lanes), f32),
        pltpu.VMEM((2, 8, lanes), f32),
        pltpu.VMEM((2, 8, lanes), f32),
        pltpu.VMEM((2, 8, lanes), f32),
        pltpu.VMEM((2 * owners, W), f32),
        pltpu.VMEM((2, W, lanes), f32),
        pltpu.VMEM((owners, 2, 2, W, lanes), bf16),
        pltpu.VMEM((owners, 2, 2, W, lanes), bf16),
        pltpu.VMEM((owners, 2, 2, 8, lanes), f32),
        dma((9,)),
        dma((2, 16)),
        dma((owners, 2)),
        dma((4, 2, 4, 2)),
        dma((2, 4, 2)),
        dma((2, 4, 2)),
        dma((2, 2)),
        dma((2, 2)),
        dma((4, 2)),
        dma((2, 2)),
        dma((5, 2)),
        dma((3, 2)),
    ]
    pairs = 2 * groups * rows * (2 * owners + 1) * W * W * 2
    shapes = (
        jax.ShapeDtypeStruct((rows, width), bf16),
        jax.ShapeDtypeStruct((rows, kv_width), bf16),
        jax.ShapeDtypeStruct((rows, kv_width), bf16),
        jax.ShapeDtypeStruct(kc.shape, f32),
        jax.ShapeDtypeStruct(vc.shape, f32),
    )
    results = pl.pallas_call(
        kernel,
        name="tail_attention_backward",
        out_shape=shapes,
        in_specs=[hbm] * 11,
        out_specs=(vmem,) * 5,
        scratch_shapes=scratch,
        cost_estimate=pl.CostEstimate(flops=5 * pairs, bytes_accessed=4 << 20, transcendentals=pairs // W),
        compiler_params=pltpu.CompilerParams(collective_id=0, has_side_effects=True, vmem_limit_bytes=50 << 20),
    )(
        *(
            pltpu.with_memory_space_constraint(v, pltpu.HBM)
            for v in (
                q, do, tk, tv, kc.reshape(2, W, kv_width), vc.reshape(2, W, kv_width),
                row_list.reshape(1, rows), read_owner, read_tile, read_list,
            )
        ),
        read_count,
    )
    return pl.pallas_call(
        write_out,
        name="write_out",
        out_shape=shapes,
        in_specs=[vmem] * 5,
        out_specs=(hbm,) * 5,
        scratch_shapes=[dma((5,))],
        compiler_params=pltpu.CompilerParams(vmem_limit_bytes=2 << 20),
    )(*results)


def solution(mesh):
    split = P(("dp", "ctx"), "tp")
    per_ctx = P(("dp", "ctx"), None)
    flat = P(("dp", "ctx"))
    return jax.shard_map(
        body,
        mesh=mesh,
        in_specs=(split,) * 6 + (flat, per_ctx, per_ctx, per_ctx, flat),
        out_specs=(split,) * 5,
        check_vma=False,
    )
```

```python
import functools
import math

import jax
import jax.numpy as jnp
from jax import lax
from jax.experimental import pallas as pl
from jax.experimental.pallas import tpu as pltpu
from jax.sharding import PartitionSpec as P

W = 128
NX = 4
NZ = 4
SCALE = 1.0 / math.sqrt(W)
LOG2E = 1.4426950408889634
SCORE_TO_LOG2 = SCALE * LOG2E
MASKED = -1e30
FLOOR = -1e29
NB = 256
f32 = jnp.float32
bf16 = jnp.bfloat16
MESH = pl.DeviceIdType.MESH
TT = (((0,), (0,)), ((), ()))

GATHER = (
    (
        (("A000", "A001", "A002", "A010", "A011", "A012",), "A00"),
        ((), "A01"),
        (("A10w", "P00w", "M00w", "A100", "A101",), "A10"),
        ((), "P00"),
        ((), "M00"),
        (("A11w", "P01w", "M01w", "A110", "A111",), "A11"),
        ((), "P01"),
        ((), "M01"),
        (("A20w", "P10w", "M10w", "A200", "A201",), "A20"),
        ((), "P10"),
        ((), "M10"),
        (("A21w", "P11w", "M11w", "A210", "A211",), "A21"),
        ((), "P11"),
        ((), "M11"),
        (("A30w", "P20w", "M20w", "A300", "A301",), "A30"),
        ((), "P20"),
        ((), "M20"),
        (("A31w", "P21w", "M21w", "M000", "M100", "A310", "A311", "P011", "P111",), "A31"),
        ((), "P21"),
        ((), "M21"),
        (("C20w", "P30w", "M30w",), "C20"),
        ((), "P30"),
        ((), "M30"),
        (("C21w", "P31w", "M31w",), "C21"),
        ((), "P31"),
        ((), "M31"),
        (("C30w", "C00w", "C01w",), "C30"),
        ((), "C00"),
        ((), "C01"),
        (("C10w", "C31w", "C11w",), "C10"),
        ((), "C31"),
        ((), "C11"),
    ),
    (
        (("A002", "A000", "A001", "A003", "A012", "A010", "A011", "A013",), "A00"),
        ((), "A01"),
        (("A10w", "A20w", "P00w", "M00w", "A102", "M000", "A100", "A101", "A203",), "A10"),
        ((), "A20"),
        ((), "P00"),
        ((), "M00"),
        (("A11w", "A21w", "P01w", "M01w", "A201", "A112", "A110", "P011", "A111", "A213",), "A11"),
        ((), "A21"),
        ((), "P01"),
        ((), "M01"),
        (("A30w", "P10w", "C00w", "C002", "A303",), "A30"),
        ((), "P10"),
        ((), "C00"),
        (("M10w", "A31w", "C01w", "M100", "A200", "A300", "C012", "A210", "A310", "A313",), "M10"),
        ((), "A31"),
        ((), "C01"),
        (("C20w", "P11w", "M11w", "A301", "C203", "P111", "A211", "A311",), "C20"),
        ((), "P11"),
        ((), "M11"),
        (("P20w", "C10w", "C21w", "C102", "C213",), "P20"),
        ((), "C10"),
        ((), "C21"),
        (("M20w", "C11w", "C112",), "M20"),
        ((), "C11"),
        (("C30w", "C303",), "C30"),
        (("P21w", "M21w",), "P21"),
        ((), "M21"),
        (("C31w", "C313",), "C31"),
        (("P30w", "M30w",), "P30"),
        ((), "M30"),
        (("P31w", "M31w",), "P31"),
        ((), "M31"),
    ),
)
SCATTER = (
    (
        ("23", ()),
        ("m3", ()),
        ("21", ()),
        ("22", ()),
        ("p3", ()),
        ("p2", ()),
        ("m2", ()),
        ("p1", ("p11",)),
        ("01", ()),
        ("03", ("030",)),
        ("20", ()),
        ("m1", ("m10", "031",)),
        ("p0", ()),
        ("m0", ()),
        ("02", ("020",)),
        ("00", ()),
        ("T0", ("021",)),
        ("U0", ("m00", "011", "010", "p01", "000", "001",)),
    ),
    (
        ("m3", ()),
        ("p0", ()),
        ("p3", ()),
        ("m0", ()),
        ("23", ("230",)),
        ("21", ()),
        ("03", ()),
        ("01", ("231",)),
        ("p2", ("210",)),
        ("m1", ()),
        ("m2", ()),
        ("22", ("211", "220", "221",)),
        ("02", ("m10",)),
        ("p1", ()),
        ("20", ("030",)),
        ("00", ("200",)),
        ("T0", ("031",)),
        ("U0", ("p11", "201", "020", "021", "010", "011", "m00", "p01", "000", "001",)),
    ),
)


def kernel(
    q_hbm, do_hbm, tk_hbm, tv_hbm, kc_hbm, vc_hbm, rl_hbm, ro_hbm, rt_hbm, rs_hbm, rc_hbm,
    gq_ref, gk_ref, gv_ref, gck_ref, gcv_ref,
    tk_ref, tv_ref, rl_ref, ro_ref, rt_ref, rs_ref, rc_ref,
    G, R1, R2, RZ2, RZ, QR, DR, QT, DT, m_ref, l_ref, c_ref, shift_ref, bias_ref, dq_ref, PS, DS, top_ref,
    in_sem, q_sem, a_recv, a_send, r1_recv, r1_send, r2_recv, r2_send, rz2_recv, rz2_send, rz_recv, rz_send,
):
    me = lax.axis_index("ctx")
    x = me // NZ
    z = me % NZ
    xp = lax.rem(x + 1, NX)
    xm = lax.rem(x + NX - 1, NX)
    x2 = lax.rem(x + 2, NX)
    inner = (z == 1) | (z == 2)
    edge = (z == 0) | (z == 3)
    low = z < 2
    zi = jnp.where(low, z + 1, z - 1)
    zo = jnp.where(low, z - 1, z + 1)
    to = [xp * NZ + z, xm * NZ + z, x * NZ + zi, x * NZ + zo]
    zk = [z, jnp.where(lax.rem(z, 2) == 0, z + 1, z - 1), jnp.where(low, 2, 1), jnp.where(low, 3, 0)]
    column = {"A": x, "P": xp, "M": xm, "C": x2, "0": x, "p": xp, "m": xm, "2": x2}
    half = 8 * W // NB

    def owner_of(group, k):
        return column[group] * NZ + zk[k]

    def by_class(ends, middle):
        pl.when(edge)(ends)
        pl.when(inner)(middle)

    def pick(n, lo, hi, leaf):
        if hi - lo == 1:
            return leaf(lo)
        mid = (lo + hi) // 2
        return lax.cond(n < mid, lambda: pick(n, lo, mid, leaf), lambda: pick(n, mid, hi, leaf))

    def send(src, dst, ssem, rsem, dev):
        pltpu.make_async_remote_copy(
            src_ref=src, dst_ref=dst, send_sem=ssem, recv_sem=rsem, device_id={"ctx": dev}, device_id_type=MESH
        ).start()

    def wait_recv(dst, rsem):
        pltpu.make_async_remote_copy(
            src_ref=dst, dst_ref=dst, send_sem=rsem, recv_sem=rsem, device_id={"ctx": to[0]}, device_id_type=MESH
        ).wait_recv()

    def wait_send(ssem):
        pltpu.make_async_remote_copy(
            src_ref=G.at[0, 0], dst_ref=G.at[0, 0], send_sem=ssem, recv_sem=ssem, device_id={"ctx": to[0]},
            device_id_type=MESH,
        ).wait_send()

    own = [
        pltpu.make_async_copy(kc_hbm, G.at[me, :, 0], in_sem.at[0]),
        pltpu.make_async_copy(vc_hbm, G.at[me, :, 1], in_sem.at[1]),
    ]
    rest = [
        pltpu.make_async_copy(src, dst, in_sem.at[i + 2])
        for i, (src, dst) in enumerate(
            (
                (tk_hbm, tk_ref), (tv_hbm, tv_ref), (rl_hbm, rl_ref),
                (ro_hbm, ro_ref), (rt_hbm, rt_ref), (rs_hbm, rs_ref), (rc_hbm, rc_ref),
            )
        )
    ]
    rest += [
        pltpu.make_async_copy(src.at[:, pl.ds(i * W, W)], dst.at[i // 8, pl.ds(i % 8 * W, W)], q_sem.at[n, i])
        for i in range(16)
        for n, (src, dst) in enumerate(((q_hbm, QR), (do_hbm, DR)))
    ]
    for copy in own:
        copy.start()

    barrier = pltpu.get_barrier_semaphore()

    def greet(dev):
        pl.semaphore_signal(barrier, inc=1, device_id={"ctx": dev}, device_id_type=MESH)

    for d in range(3):
        greet(to[d])
    pl.when(inner)(lambda: greet(to[3]))
    for copy in rest:
        copy.start()
    for copy in own:
        copy.wait()
    by_class(lambda: pl.semaphore_wait(barrier, 3), lambda: pl.semaphore_wait(barrier, 4))

    def gather_op(op):
        group, k, a = op[0], int(op[1]), int(op[2])
        owner = owner_of(group, k)
        tile = G.at[owner, a]
        if op[3] == "w":
            wait_recv(tile, a_recv.at[owner, a])
        else:
            d = int(op[3])
            send(tile, tile, a_send.at[d, 0 if group == "A" else 1, k, a], a_recv.at[owner, a], to[d])

    def gather_ops(cls, n):
        for op in GATHER[cls][n][0]:
            gather_op(op)

    by_class(lambda: gather_ops(0, 0), lambda: gather_ops(1, 0))

    for copy in rest:
        copy.wait()
    for h in range(2):
        for j in range(8):
            rows = slice(j * W, (j + 1) * W)
            QT[h, :, rows] = QR[h, rows, :].T
            DT[h, :, rows] = DR[h, rows, :].T
    reads = ro_ref.shape[1]
    tid = ro_ref[...] * 2 + rt_ref[...]
    live = lax.broadcasted_iota(jnp.int32, (1, reads), 1) < rc_ref[0]
    tid = jnp.where(live, tid, -1)
    named = lax.broadcasted_iota(jnp.int32, (2 * NX * NZ, reads), 0) == tid
    count0 = jnp.sum(jnp.where(named & (rs_ref[...] == 0), 1.0, 0.0), axis=1, keepdims=True)
    count1 = jnp.sum(jnp.where(named & (rs_ref[...] == 1), 1.0, 0.0), axis=1, keepdims=True)
    rl = rl_ref[...]
    times = jnp.where(rl == 0, count0, count1)
    bias_ref[...] = jnp.where(times > 0.5, jnp.log2(jnp.maximum(times, 1.0)), MASKED)
    cut = jnp.sum(jnp.where(rl == 0, 1.0, 0.0), axis=1, keepdims=True)
    key_at = lax.broadcasted_iota(jnp.int32, (W, W), 0)
    row_at = lax.broadcasted_iota(jnp.int32, (W, W), 1)
    tail_ok = (key_at <= row_at) & jnp.logical_not((key_at.astype(f32) < cut) & (row_at.astype(f32) >= cut))
    tail_ok = jnp.concatenate([tail_ok.astype(f32)] * (NB // W), axis=1) > 0.5

    for h in range(2):
        hs = slice(h * W, (h + 1) * W)
        for j in range(half):
            sl = slice(j * NB, (j + 1) * NB)
            s = jnp.dot(tk_ref[:, hs], QT[h, :, sl], preferred_element_type=f32)
            dp = jnp.dot(tv_ref[:, hs], DT[h, :, sl], preferred_element_type=f32)
            t = jnp.where(tail_ok, s * SCORE_TO_LOG2, MASKED).reshape(16, 8, NB)
            top = jnp.maximum(jnp.max(t, axis=0), FLOOR)
            e = jnp.exp2(t - top[None])
            low_sum = jnp.sum(e, axis=0)
            cross = jnp.sum(e * dp.reshape(16, 8, NB), axis=0)
            part = jnp.exp2(top - jnp.max(top, axis=0, keepdims=True))
            mean = jnp.sum(cross * part, axis=0, keepdims=True) / jnp.sum(low_sum * part, axis=0, keepdims=True)
            mean = jnp.broadcast_to(mean, (8, NB))
            m_ref[h, :, sl] = top
            l_ref[h, :, sl] = low_sum
            c_ref[h, :, sl] = cross - mean * low_sum
            shift_ref[h, :, sl] = mean

    def stats_tile(owner, a):
        b = jnp.broadcast_to(bias_ref[pl.ds(owner * 2 + a, 1), :], (8, W))
        b = jnp.concatenate([b] * (NB // W), axis=1)
        for h in range(2):
            hs = slice(h * W, (h + 1) * W)
            for j in range(half):
                sl = slice(j * NB, (j + 1) * NB)
                s = jnp.dot(G[owner, a, 0, :, hs], QT[h, :, sl], preferred_element_type=f32)
                dp = jnp.dot(G[owner, a, 1, :, hs], DT[h, :, sl], preferred_element_type=f32)
                t = (s * SCORE_TO_LOG2).reshape(16, 8, NB)
                old = m_ref[h, :, sl]
                new = jnp.maximum(old, jnp.max(t, axis=0) + b)
                fade = jnp.exp2(old - new)
                e = jnp.exp2(t - (new - b)[None])
                dlow = (dp.reshape(16, 8, NB) - shift_ref[h, :, sl][None]).astype(bf16)
                PS[owner, h, a, :, sl] = e.reshape(W, NB).astype(bf16)
                DS[owner, h, a, :, sl] = dlow.reshape(W, NB)
                top_ref[owner, a, h, :, sl] = new
                m_ref[h, :, sl] = new
                l_ref[h, :, sl] = l_ref[h, :, sl] * fade + jnp.sum(e, axis=0)
                c_ref[h, :, sl] = c_ref[h, :, sl] * fade + jnp.sum(e * dlow.astype(f32), axis=0)

    def gather_leaf(cls):
        def leaf(n):
            if n > 0:
                gather_ops(cls, n)
            op = GATHER[cls][n][1]
            return owner_of(op[0], int(op[1])) * 2 + int(op[2])

        return leaf

    def gather_step(n, carry):
        at = lax.cond(
            inner, lambda: pick(n, 0, 2 * NX * NZ, gather_leaf(1)), lambda: pick(n, 0, 2 * NX * NZ, gather_leaf(0))
        )
        stats_tile(at // 2, at % 2)
        return carry

    lax.fori_loop(0, 2 * NX * NZ, gather_step, 0)

    for h in range(2):
        m = m_ref[h]
        top = jnp.max(m, axis=0, keepdims=True)
        part = jnp.exp2(m - top)
        total = jnp.sum(l_ref[h] * part, axis=0, keepdims=True)
        cross = jnp.sum(c_ref[h] * part, axis=0, keepdims=True)
        m_ref[h] = jnp.broadcast_to(top + jnp.log2(total), (8, 8 * W))
        c_ref[h] = jnp.broadcast_to(cross / total, (8, 8 * W))
        dq_ref[h] = jnp.zeros((W, 8 * W), f32)

    def gather_left(cls):
        for ops, _ in GATHER[cls]:
            for op in ops:
                if op[3] != "w":
                    wait_send(a_send.at[int(op[3]), 0 if op[0] == "A" else 1, int(op[1]), int(op[2])])

    by_class(lambda: gather_left(0), lambda: gather_left(1))

    def grads_chunk(owner):
        for h in range(2):
            hs = slice(h * W, (h + 1) * W)
            for a in range(2):
                for j in range(half):
                    sl = slice(j * NB, (j + 1) * NB)
                    f = jnp.exp2(top_ref[owner, a, h, :, sl] - m_ref[h, :, sl])
                    p = PS[owner, h, a, :, sl].astype(f32).reshape(16, 8, NB) * f[None]
                    d = p * (DS[owner, h, a, :, sl].astype(f32).reshape(16, 8, NB) - c_ref[h, :, sl][None])
                    PS[owner, h, a, :, sl] = p.reshape(W, NB).astype(bf16)
                    DS[owner, h, a, :, sl] = d.reshape(W, NB).astype(bf16)
            d_all = DS[owner, h].reshape(2 * W, 8 * W)
            keys = jnp.concatenate([G[owner, 0, 0, :, hs], G[owner, 1, 0, :, hs]], axis=0)
            dq_ref[h] += lax.dot_general(keys, d_all, TT, preferred_element_type=f32)
            dv = jnp.dot(PS[owner, h].reshape(2 * W, 8 * W), DR[h], preferred_element_type=f32)
            dk = jnp.dot(d_all, QR[h], preferred_element_type=f32) * SCALE
            for a in range(2):
                rows = slice(a * W, (a + 1) * W)
                G[owner, a, 0, :, hs] = dk[rows].astype(bf16)
                G[owner, a, 1, :, hs] = dv[rows].astype(bf16)

    def merge(ref, parts):
        def rows_of(i, carry):
            r = pl.ds(pl.multiple_of(i * 32, 32), 32)
            total = ref[:, r, :].astype(f32)
            for part in parts:
                total = total + part[:, r, :].astype(f32)
            ref[:, r, :] = total.astype(bf16)
            return carry

        lax.fori_loop(0, W // 32, rows_of, 0)

    def route(cls, group, k, a):
        needs = []
        if group == "2":
            if cls:
                needs.append((RZ2.at[k, a], rz2_recv.at[k, a]))
            if k >= 2:
                slot = k - 2 if cls else k
                return needs, 2, rz2_send.at[k - 2, a], RZ2.at[slot, a], rz2_recv.at[slot, a]
            return needs, 1 - a, r2_send.at[k, a], R2.at[k, a], r2_recv.at[k, a]
        if group in "mp":
            d = "mp".index(group)
            if k < 2 and a == d:
                needs.append((R2.at[k, a], r2_recv.at[k, a]))
            return needs, 1 - d, r1_send.at[d, k, a], R1.at[d, k, a], r1_recv.at[d, k, a]
        needs += [(R1.at[d, k, a], r1_recv.at[d, k, a]) for d in range(2)]
        if k == 0:
            needs += [(RZ.at[slot, a], rz_recv.at[slot, a]) for slot in ((0, 4) if cls else (0,))]
            return needs, None, None, None, None
        if cls:
            needs.append((RZ.at[k, a], rz_recv.at[k, a]))
            slot = 0 if k == 1 else k - 2
        else:
            slot = 4 if k == 1 else k
        return needs, 3 if cls and k == 1 else 2, rz_send.at[k - 1, a], RZ.at[slot, a], rz_recv.at[slot, a]

    def pass_on(cls, group, k, a):
        owner = owner_of(group, k)
        needs, d, ssem, there, rsem = route(cls, group, k, a)
        for ref, sem in needs:
            wait_recv(ref, sem)
        if d is None:
            rows = slice(a * W, (a + 1) * W)
            for i, out in enumerate((gck_ref, gcv_ref)):
                total = G[owner, a, i].astype(f32)
                for ref, _ in needs:
                    total = total + ref[i].astype(f32)
                out[rows, :] = total
            return
        if needs:
            merge(G.at[owner, a], [ref for ref, _ in needs])
        send(G.at[owner, a], there, ssem, rsem, to[d])

    def after_chunk(cls, n):
        chunk, posts = SCATTER[cls][n]
        if chunk[0] not in "TU":
            for a in range(2):
                if not route(cls, chunk[0], int(chunk[1]), a)[0]:
                    pass_on(cls, chunk[0], int(chunk[1]), a)
        for post in posts:
            pass_on(cls, post[0], int(post[1]), int(post[2]))

    def chunk_leaf(cls):
        return lambda n: owner_of(SCATTER[cls][n][0][0], int(SCATTER[cls][n][0][1]))

    def after_leaf(cls):
        def leaf(n):
            after_chunk(cls, n)

        return leaf

    def scatter_step(n, carry):
        owner = lax.cond(
            inner, lambda: pick(n, 0, NX * NZ, chunk_leaf(1)), lambda: pick(n, 0, NX * NZ, chunk_leaf(0))
        )
        grads_chunk(owner)
        by_class(lambda: pick(n, 0, NX * NZ, after_leaf(0)), lambda: pick(n, 0, NX * NZ, after_leaf(1)))
        return carry

    lax.fori_loop(0, NX * NZ, scatter_step, 0)

    for h in range(2):
        hs = slice(h * W, (h + 1) * W)
        for j in range(half):
            sl = slice(j * NB, (j + 1) * NB)
            s = jnp.dot(tk_ref[:, hs], QT[h, :, sl], preferred_element_type=f32)
            dp = jnp.dot(tv_ref[:, hs], DT[h, :, sl], preferred_element_type=f32)
            t = jnp.where(tail_ok, s * SCORE_TO_LOG2, MASKED).reshape(16, 8, NB)
            p = jnp.exp2(t - m_ref[h, :, sl][None])
            d = p * (dp.reshape(16, 8, NB) - (c_ref[h, :, sl] + shift_ref[h, :, sl])[None])
            PS[0, h, 0, :, sl] = p.reshape(W, NB).astype(bf16)
            DS[0, h, 0, :, sl] = d.reshape(W, NB).astype(bf16)
        gv_ref[:, hs] = jnp.dot(PS[0, h, 0], DR[h], preferred_element_type=f32).astype(bf16)
        gk_ref[:, hs] = (jnp.dot(DS[0, h, 0], QR[h], preferred_element_type=f32) * SCALE).astype(bf16)
        dq_ref[h] += lax.dot_general(tk_ref[:, hs], DS[0, h, 0], TT, preferred_element_type=f32)
    by_class(lambda: after_chunk(0, NX * NZ), lambda: after_chunk(1, NX * NZ))
    for h in range(2):
        for j in range(8):
            gq_ref[:, (h * 8 + j) * W : (h * 8 + j + 1) * W] = (
                (dq_ref[h, :, j * W : (j + 1) * W] * SCALE).T.astype(bf16)
            )
    by_class(lambda: after_chunk(0, NX * NZ + 1), lambda: after_chunk(1, NX * NZ + 1))

    def sums_left(cls):
        for group in "2mp0":
            for k in range(4):
                for a in range(2):
                    if group + str(k) != "00":
                        wait_send(route(cls, group, k, a)[2])


    by_class(lambda: sums_left(0), lambda: sums_left(1))


def write_out(*refs):
    n = len(refs) // 2
    sem = refs[-1]
    copies = [pltpu.make_async_copy(refs[i], refs[n + i], sem.at[i]) for i in range(n)]
    for copy in copies:
        copy.start()
    for copy in copies:
        copy.wait()


def body(q, do, tk, tv, kc, vc, row_list, read_owner, read_tile, read_list, read_count):
    rows, width = q.shape
    kv_width = tk.shape[1]
    groups = width // kv_width
    reads = read_owner.shape[1]
    owners = NX * NZ
    vmem = pl.BlockSpec(memory_space=pltpu.VMEM)
    hbm = pl.BlockSpec(memory_space=pl.ANY)
    tile = (2, W, kv_width)
    lanes = groups * W
    dma = pltpu.SemaphoreType.DMA
    scratch = [
        pltpu.VMEM((rows, kv_width), bf16),
        pltpu.VMEM((rows, kv_width), bf16),
        pltpu.VMEM((1, rows), jnp.int32),
        pltpu.VMEM((1, reads), jnp.int32),
        pltpu.VMEM((1, reads), jnp.int32),
        pltpu.VMEM((1, reads), jnp.int32),
        pltpu.SMEM((1,), jnp.int32),
        pltpu.VMEM((owners, 2) + tile, bf16),
        pltpu.VMEM((2, 4, 2) + tile, bf16),
        pltpu.VMEM((2, 2) + tile, bf16),
        pltpu.VMEM((4, 2) + tile, bf16),
        pltpu.VMEM((5, 2) + tile, bf16),
        pltpu.VMEM((2, lanes, W), bf16),
        pltpu.VMEM((2, lanes, W), bf16),
        pltpu.VMEM((2, W, lanes), bf16),
        pltpu.VMEM((2, W, lanes), bf16),
        pltpu.VMEM((2, 8, lanes), f32),
        pltpu.VMEM((2, 8, lanes), f32),
        pltpu.VMEM((2, 8, lanes), f32),
        pltpu.VMEM((2, 8, lanes), f32),
        pltpu.VMEM((2 * owners, W), f32),
        pltpu.VMEM((2, W, lanes), f32),
        pltpu.VMEM((owners, 2, 2, W, lanes), bf16),
        pltpu.VMEM((owners, 2, 2, W, lanes), bf16),
        pltpu.VMEM((owners, 2, 2, 8, lanes), f32),
        dma((9,)),
        dma((2, 16)),
        dma((owners, 2)),
        dma((4, 2, 4, 2)),
        dma((2, 4, 2)),
        dma((2, 4, 2)),
        dma((2, 2)),
        dma((2, 2)),
        dma((4, 2)),
        dma((2, 2)),
        dma((5, 2)),
        dma((3, 2)),
    ]
    pairs = 2 * groups * rows * (2 * owners + 1) * W * W * 2
    shapes = (
        jax.ShapeDtypeStruct((rows, width), bf16),
        jax.ShapeDtypeStruct((rows, kv_width), bf16),
        jax.ShapeDtypeStruct((rows, kv_width), bf16),
        jax.ShapeDtypeStruct(kc.shape, f32),
        jax.ShapeDtypeStruct(vc.shape, f32),
    )
    results = pl.pallas_call(
        kernel,
        name="tail_attention_backward",
        out_shape=shapes,
        in_specs=[hbm] * 11,
        out_specs=(vmem,) * 5,
        scratch_shapes=scratch,
        cost_estimate=pl.CostEstimate(flops=5 * pairs, bytes_accessed=4 << 20, transcendentals=pairs // W),
        compiler_params=pltpu.CompilerParams(collective_id=0, has_side_effects=True, vmem_limit_bytes=50 << 20),
    )(
        *(
            pltpu.with_memory_space_constraint(v, pltpu.HBM)
            for v in (
                q, do, tk, tv, kc.reshape(2, W, kv_width), vc.reshape(2, W, kv_width),
                row_list.reshape(1, rows), read_owner, read_tile, read_list,
            )
        ),
        read_count,
    )
    return pl.pallas_call(
        write_out,
        name="write_out",
        out_shape=shapes,
        in_specs=[vmem] * 5,
        out_specs=(hbm,) * 5,
        scratch_shapes=[dma((5,))],
        compiler_params=pltpu.CompilerParams(vmem_limit_bytes=2 << 20),
    )(*results)


def solution(mesh):
    split = P(("dp", "ctx"), "tp")
    per_ctx = P(("dp", "ctx"), None)
    flat = P(("dp", "ctx"))
    return jax.shard_map(
        body,
        mesh=mesh,
        in_specs=(split,) * 6 + (flat, per_ctx, per_ctx, per_ctx, flat),
        out_specs=(split,) * 5,
        check_vma=False,
    )
```
